32 devices in a mesh: dp: 16 (over z, x, core), seq: 2 (over y).
Axes of the slice: x: 2, y: 2, z: 4, core: 2. Of those that a mesh axis runs over, the one named last changes fastest.
Arguments:
- hidden: bfloat16 [32, 512, 768], P('dp', 'seq'), may hold values from -6 to 6
- encoded: bfloat16 [32, 1024, 768], P('dp', 'seq'), may hold values from -6 to 6
- cotangent: bfloat16 [32, 512, 768], P('dp', 'seq'), may hold values from -6 to 6
- w_self_qkv: bfloat16 [768, 2304], P(('dp', 'seq')), may hold values from -0.21875 to 0.21875
- w_self_out: bfloat16 [768, 768], P(('dp', 'seq')), may hold values from -0.625 to 0.625
- w_cross_q: bfloat16 [768, 768], P(('dp', 'seq')), may hold values from -0.21875 to 0.21875
- w_cross_kv: bfloat16 [768, 1536], P(('dp', 'seq')), may hold values from -0.21875 to 0.21875
- w_cross_out: bfloat16 [768, 768], P(('dp', 'seq')), may hold values from -0.625 to 0.625
- w_ffn_in: bfloat16 [768, 3072], P(('dp', 'seq')), may hold values from -0.21875 to 0.21875
- w_ffn_out: bfloat16 [3072, 768], P(('dp', 'seq')), may hold values from -0.15625 to 0.15625
- norm_gains: float32 [3, 768], replicated, may hold values from 0.5 to 1.5
- bucket_bias_matrix: float32 [32, 12], replicated, may hold values from -4 to 4
- dec_lengths: int32 [32], P('dp'), may hold values from 1 to 512, as said below
- ident_tags: int32 [32, 512], P('dp', 'seq'), may hold values 0 or 1
- ident_mask: int32 [32, 1024], P('dp'), may hold values from 0 to 1, as said below
- bucket_ids: int32 [512, 512], P('seq'), may hold values from 0 to 31, as said below
Outputs:
- block_out: bfloat16 [32, 512, 768], P('dp', 'seq')
- grad_hidden: bfloat16 [32, 512, 768], P('dp', 'seq')
- grad_encoded: bfloat16 [32, 1024, 768], P('dp', 'seq')
- grad_self_qkv: float32 [768, 2304], P(('dp', 'seq'))
- grad_self_out: float32 [768, 768], P(('dp', 'seq'))
- grad_cross_q: float32 [768, 768], P(('dp', 'seq'))
- grad_cross_kv: float32 [768, 1536], P(('dp', 'seq'))
- grad_cross_out: float32 [768, 768], P(('dp', 'seq'))
- grad_ffn_in: float32 [768, 3072], P(('dp', 'seq'))
- grad_ffn_out: float32 [3072, 768], P(('dp', 'seq'))
- grad_gains: float32 [3, 768], replicated
- grad_table: float32 [32, 12], replicated
The draws below stay inside these ranges and needn't reach their ends.
Inputs may be any that keep to these rules, and one draw needn't show every extreme that they name: `dec_lengths`: in each aligned block of 2 items at least one item has length 512. `ident_mask`: in every aligned run of 8 encoder positions of an item at least one entry is 1. `bucket_ids`: causal T5 buckets (16 exact, then logarithmic up to a distance of 128) of the distance between the token places of the query and the key, 0 where the key's place is after the query's.
All inputs are finite; a program needn't handle non-finite values. No bound on the sum of `ident_tags` on one device may be relied on, other than what follows from the above.
Results may differ from the reference program's by a relative error of at most 0.02.
Values may be sent and summed in bfloat16 or wider, within the bound.
A program may use at most 256 MiB of HBM per device.

```python
import math
import jax
import jax.numpy as jnp
from jax import lax

D = 768
HEADS = 12
HEAD_DIM = 64
FF = 3072
BUCKETS = 32
DEC_LEN = 512
ENC_LEN = 1024
ITEMS_DEV = 2
ITEMS = 32


def draw_dec_lengths(key, part):
    key = jax.random.fold_in(key, 11)
    key_shift, key_cut, key_pick = jax.random.split(key, 3)
    shift = jax.random.randint(key_shift, (ITEMS,), 0, 4)
    base = DEC_LEN // jnp.power(2, shift)
    cut = jax.random.randint(key_cut, (ITEMS,), 0, 1 << 20) % (base // 2 + 1)
    lengths = jnp.maximum(base - cut, 1)
    groups = ITEMS // ITEMS_DEV
    pick = jax.random.randint(key_pick, (groups,), 0, ITEMS_DEV)
    index = jnp.arange(ITEMS)
    chosen = index % ITEMS_DEV == pick[index // ITEMS_DEV]
    return jnp.where(chosen, DEC_LEN, lengths).astype(jnp.int32)


def draw_ident_mask(key, part):
    key = jax.random.fold_in(key, 12)
    key_marks, key_offset = jax.random.split(key, 2)
    marks = jax.random.randint(key_marks, (ITEMS, ENC_LEN), 0, 5) < 2
    offset = jax.random.randint(key_offset, (ITEMS, ENC_LEN // 8, 1), 0, 8)
    forced = (jnp.arange(8)[None, None, :] == offset).reshape(ITEMS, ENC_LEN)
    return (marks | forced).astype(jnp.int32)


def draw_bucket_ids(key, part):
    key = jax.random.fold_in(key, 13)
    key_gaps, key_jump = jax.random.split(key, 2)
    gaps = jax.random.randint(key_gaps, (DEC_LEN,), 1, 4)
    jump = jax.random.randint(key_jump, (), 1, DEC_LEN)
    gaps = jnp.where(jnp.arange(DEC_LEN) == jump, 160, gaps)
    places = jnp.cumsum(gaps)
    distance = jnp.maximum(places[:, None] - places[None, :], 0)
    bounds = jnp.array([int(math.ceil(16 * 8 ** (step / 16))) for step in range(1, 16)], jnp.int32)
    far_bucket = 16 + jnp.sum((distance[:, :, None] >= bounds[None, None, :]).astype(jnp.int32), axis=-1)
    return jnp.where(distance < 16, distance, far_bucket).astype(jnp.int32)


def touch_ends(values, stream_key, low, high):
    index_at = [jax.random.randint(jax.random.fold_in(stream_key, axis), (), 0, length) for axis, length in enumerate(values.shape)]
    widest = values.shape.index(max(values.shape))
    neighbour = index_at[:widest] + [(index_at[widest] + 1) % values.shape[widest]] + index_at[widest + 1:]
    return values.at[tuple(index_at)].set(low).at[tuple(neighbour)].set(high)


def level_of(own_key, dims, cuts, smallest, top_value):
    def one(position, shards_of):
        draws = jax.random.uniform(jax.random.fold_in(jax.random.fold_in(own_key, 6), position), (shards_of,), jnp.float32, smallest / len(cuts), top_value / len(cuts))
        return jnp.repeat(jnp.exp(draws), dims[position] // shards_of).reshape((-1,) + (1,) * (len(dims) - position - 1))

    loudness = one(*cuts[0])
    for cut in cuts[1:]:
        loudness = loudness * one(*cut)
    return loudness


def gaussian(own_key, dims, deviation, limit, cuts=(), dtype=jnp.bfloat16):
    loudness = level_of(own_key, dims, cuts, -0.22, 0.18) if cuts else 1.0
    values = jax.random.normal(own_key, dims, jnp.float32) * deviation * loudness
    return jnp.minimum(jnp.maximum(values, -limit), limit).astype(dtype)


def setup_inputs(seed: int = 0) -> dict:
    streams_of = jax.random.split(jax.random.key(seed), 17)
    hidden = gaussian(streams_of[0], (ITEMS, DEC_LEN, D), 1.0, 6.0, ((0, 16), (1, 2)))
    encoded = gaussian(streams_of[1], (ITEMS, ENC_LEN, D), 1.0, 6.0, ((0, 16), (1, 2)))
    cotangent = gaussian(streams_of[2], (ITEMS, DEC_LEN, D), 1.0, 6.0, ((0, 16), (1, 2)))
    w_self_qkv = gaussian(streams_of[3], (D, 3 * D), D ** -0.5, 0.21875, ((0, 32),))
    w_self_out = gaussian(streams_of[4], (D, D), (D // 8) ** -0.5, 0.625, ((0, 32),))
    w_cross_q = gaussian(streams_of[5], (D, D), D ** -0.5, 0.21875, ((0, 32),))
    w_cross_kv = gaussian(streams_of[6], (D, 2 * D), D ** -0.5, 0.21875, ((0, 32),))
    w_cross_out = gaussian(streams_of[7], (D, D), (D // 8) ** -0.5, 0.625, ((0, 32),))
    w_ffn_in = gaussian(streams_of[8], (D, FF), D ** -0.5, 0.21875, ((0, 32),))
    w_ffn_out = gaussian(streams_of[9], (FF, D), (FF // 2) ** -0.5, 0.15625, ((0, 32),))
    norm_gains = jnp.clip(1.0 + 0.1 * jax.random.normal(streams_of[10], (3, D), jnp.float32), 0.5, 1.5)
    bucket_bias_matrix = gaussian(streams_of[11], (BUCKETS, HEADS), 1.0, 4.0, (), jnp.float32)
    dec_lengths = draw_dec_lengths(jax.random.fold_in(streams_of[16], 71), 0)
    ident_tags = touch_ends((jax.random.randint(streams_of[13], (ITEMS, DEC_LEN), 0, 3) < 1).astype(jnp.int32), jax.random.fold_in(streams_of[13], 1), 0, 1)
    ident_mask = draw_ident_mask(jax.random.fold_in(streams_of[16], 71), 0)
    bucket_ids = draw_bucket_ids(jax.random.fold_in(streams_of[16], 71), 0)
    return {"hidden": hidden, "encoded": encoded, "cotangent": cotangent, "w_self_qkv": w_self_qkv, "w_self_out": w_self_out, "w_cross_q": w_cross_q, "w_cross_kv": w_cross_kv, "w_cross_out": w_cross_out, "w_ffn_in": w_ffn_in, "w_ffn_out": w_ffn_out, "norm_gains": norm_gains, "bucket_bias_matrix": bucket_bias_matrix, "dec_lengths": dec_lengths, "ident_tags": ident_tags, "ident_mask": ident_mask, "bucket_ids": bucket_ids}


epsilon = 1e-06
score_scale = 0.125
masked_score = -1e+30
gelu_coeff = 0.7978845608028654
cubic_coeff = 0.044715

@jax.custom_vjp
def low(v):
    return lax.optimization_barrier(v.astype(jnp.bfloat16)).astype(jnp.float32)

@jax.custom_vjp
def low_back(v):
    return v

def low_keep(v):
    return (low(v), None)

def low_pass(kept, grad):
    return (grad,)

def back_keep(v):
    return (v, None)

def back_low(kept, grad):
    return (low(grad),)
low.defvjp(low_keep, low_pass)
low_back.defvjp(back_keep, back_low)

def rounded_both(values):
    return low(low_back(values))

def rms_norm(values, gain):
    return values * lax.rsqrt(lax.optimization_barrier(jnp.mean(values * values, axis=-1, keepdims=True)) + epsilon) * gain

def smooth_gelu(values):
    return 0.5 * values * (1.0 + jnp.tanh(gelu_coeff * (values + cubic_coeff * values * values * values)))

def matmul(left, right):
    return jnp.dot(left, right, precision=lax.Precision.HIGHEST)

def split_heads(values):
    return values.reshape(values.shape[0], values.shape[1] // HEAD_DIM, HEAD_DIM)

def attend(query, keys, values, bias, mask):
    scores = jnp.einsum('qhe,khe->hqk', split_heads(query), split_heads(keys), precision=lax.Precision.HIGHEST) * score_scale
    scores = low_back(scores + bias)
    scores = jnp.where(mask[None], scores, masked_score)
    top = lax.optimization_barrier(jnp.max(scores, axis=-1, keepdims=True))
    expo = jnp.exp(scores - top)
    probs = low(expo / lax.optimization_barrier(jnp.sum(expo, axis=-1, keepdims=True)))
    output = jnp.einsum('hqk,khe->qhe', probs, split_heads(values), precision=lax.Precision.HIGHEST)
    return output.reshape(query.shape[0], query.shape[1])

def forward(inputs, encoder, w_qkv, w_so, w_cq, w_ckv, w_co, w_in, w_out, gains, table, length, tags, imask, bucket_ids):
    positions = jnp.arange(DEC_LEN)
    self_mask = (positions[None, :] <= positions[:, None]) & (positions[None, :] < length)
    cross_mask = (tags[:, None] == 0) | (imask[None, :] == 1)
    bias = jnp.transpose(table[bucket_ids], (2, 0, 1))
    normed = low(rms_norm(inputs, gains[0]))
    qkv = rounded_both(matmul(normed, w_qkv))
    attended = rounded_both(attend(qkv[:, :D], qkv[:, D:2 * D], qkv[:, 2 * D:], bias, self_mask))
    after_self = inputs + low_back(matmul(attended, w_so))
    normed_two = low(rms_norm(after_self, gains[1]))
    cross_query = rounded_both(matmul(normed_two, w_cq))
    cross_kv = rounded_both(matmul(encoder, w_ckv))
    cross_att = rounded_both(attend(cross_query, cross_kv[:, :D], cross_kv[:, D:], 0.0, cross_mask))
    after_cross = after_self + low_back(matmul(cross_att, w_co))
    normed_three = low(rms_norm(after_cross, gains[2]))
    pre = low_back(matmul(normed_three, w_in))
    act = rounded_both(smooth_gelu(pre))
    return after_cross + low_back(matmul(act, w_out))

def reference(hidden, encoded, cotangent, w_self_qkv, w_self_out, w_cross_q, w_cross_kv, w_cross_out, w_ffn_in, w_ffn_out, norm_gains, bucket_bias_matrix, dec_lengths, ident_tags, ident_mask, bucket_ids):
    params = tuple((w.astype(jnp.float32) for w in (w_self_qkv, w_self_out, w_cross_q, w_cross_kv, w_cross_out, w_ffn_in, w_ffn_out)))
    params = params + (norm_gains.astype(jnp.float32), bucket_bias_matrix.astype(jnp.float32))
    zeros = jax.tree.map(jnp.zeros_like, params)

    def step(totals, item):
        inputs, encoder, grad_out, length, tags, imask = item

        def apply(inputs_f, encoder_f, *weights):
            return forward(inputs_f, encoder_f, *weights, length, tags, imask, bucket_ids)
        result, pull = jax.vjp(apply, inputs.astype(jnp.float32), encoder.astype(jnp.float32), *params)
        grads = pull(grad_out.astype(jnp.float32))
        totals = jax.tree.map(lambda left, right: left + right, totals, tuple(grads[2:]))
        return (totals, (result.astype(jnp.bfloat16), grads[0].astype(jnp.bfloat16), grads[1].astype(jnp.bfloat16)))
    totals, (block_out, grad_hidden, grad_encoded) = lax.scan(step, zeros, (hidden, encoded, cotangent, dec_lengths, ident_tags, ident_mask))
    return (block_out, grad_hidden, grad_encoded, totals[0], totals[1], totals[2], totals[3], totals[4], totals[5], totals[6], totals[7], totals[8])
```

```python
import functools
import itertools
import typing

import jax
import jax.numpy as jnp
from jax import lax
from jax.experimental import pallas as pl
from jax.experimental.pallas import tpu as pltpu
from jax.sharding import PartitionSpec as P

epsilon = 1e-06
score_scale = 0.125
masked_score = -1e30
gelu_coeff = 0.7978845608028654
cubic_coeff = 0.044715


def rms_norm(values, gain):
    return values * lax.rsqrt(jnp.mean(values * values, axis=-1, keepdims=True) + epsilon) * gain


def smooth_gelu(values):
    return (
        0.5
        * values
        * (1.0 + jnp.tanh(gelu_coeff * (values + cubic_coeff * values * values * values)))
    )


def matmul(left, right):
    return jnp.dot(left, right, preferred_element_type=jnp.float32)


def contract_rows(left, right):
    return lax.dot_general(
        left, right, (((0,), (0,)), ((), ())), preferred_element_type=jnp.float32
    )


def contract_cols(left, right):
    return lax.dot_general(
        left, right, (((1,), (1,)), ((), ())), preferred_element_type=jnp.float32
    )


def masked_scores(query, keys, bias, mask):
    scores = (
        jnp.einsum("iqhe,ikhe->ihqk", query, keys, preferred_element_type=jnp.float32) * score_scale
    )
    scores = scores + bias
    return jnp.where(mask[:, None], scores, masked_score)


def attend_forward(query, keys, values, bias, mask):
    scores = masked_scores(query, keys, bias, mask)
    top = jnp.max(scores, axis=-1, keepdims=True)
    expo = jnp.exp(scores - top)
    total = jnp.sum(expo, axis=-1, keepdims=True)
    probs = (expo / total).astype(jnp.bfloat16)
    output = jnp.einsum("ihqk,ikhe->iqhe", probs, values, preferred_element_type=jnp.float32)
    return (output.astype(jnp.bfloat16), top + jnp.log(total))


def attend_backward(query, keys, values, bias, mask, log_total, grad_out):
    probs = jnp.exp(masked_scores(query, keys, bias, mask) - log_total)
    grad_probs = jnp.einsum("iqhe,ikhe->ihqk", grad_out, values, preferred_element_type=jnp.float32)
    grad_values = jnp.einsum(
        "ihqk,iqhe->ikhe", probs.astype(jnp.bfloat16), grad_out, preferred_element_type=jnp.float32
    )
    inner = jnp.sum(grad_probs * probs, axis=-1, keepdims=True)
    grad_scores = (probs * (grad_probs - inner)).astype(jnp.bfloat16)
    grad_query = (
        jnp.einsum("ihqk,ikhe->iqhe", grad_scores, keys, preferred_element_type=jnp.float32)
        * score_scale
    )
    grad_keys = (
        jnp.einsum("ihqk,iqhe->ikhe", grad_scores, query, preferred_element_type=jnp.float32)
        * score_scale
    )
    return (grad_query, grad_keys, grad_values, grad_scores)


def split_body(
    hidden,
    encoded,
    cotangent,
    w_self_qkv,
    w_self_out,
    w_cross_q,
    w_cross_kv,
    w_cross_out,
    w_ffn_in,
    w_ffn_out,
    norm_gains,
    bucket_bias_matrix,
    dec_lengths,
    ident_tags,
    ident_mask,
    bucket_ids,
):
    items, local_dec, width = hidden.shape
    local_enc = encoded.shape[1]
    heads = bucket_bias_matrix.shape[1]
    head_dim = width // heads
    bucket_count = bucket_bias_matrix.shape[0]
    full_dec = local_dec * lax.axis_size("seq")
    full_enc = local_enc * lax.axis_size("seq")
    device_count = lax.axis_size("dp") * lax.axis_size("seq")
    query_pos = lax.axis_index("seq") * local_dec + jnp.arange(local_dec)
    key_pos = jnp.arange(full_dec)
    self_mask = (key_pos[None, None, :] <= query_pos[None, :, None]) & (
        key_pos[None, None, :] < dec_lengths[:, None, None]
    )
    cross_mask = (ident_tags[:, :, None] == 0) | (ident_mask[:, None, :] == 1)
    bucket_indicator = (bucket_ids[None, :, :] == jnp.arange(bucket_count)[:, None, None]).astype(
        jnp.float32
    )
    self_attention_bias = jnp.einsum(
        "ufp,uo->ofp", bucket_indicator, bucket_bias_matrix, precision=lax.Precision.HIGHEST
    )
    inputs = hidden.reshape(-1, width).astype(jnp.float32)
    enc_rows = encoded.reshape(-1, width)

    def forward_pass(weights):
        wqkv, wso, wcq, wckv, wco, win, wout = weights
        normed = rms_norm(inputs, norm_gains[0]).astype(jnp.bfloat16)
        qkv = matmul(normed, wqkv).astype(jnp.bfloat16)
        query = qkv[:, :width].reshape(items, local_dec, heads, head_dim)
        local_kv = qkv[:, width:].reshape(items, local_dec, 2 * width)
        all_kv = lax.all_gather(local_kv, "seq", axis=1, tiled=True)
        keys = all_kv[:, :, :width].reshape(items, full_dec, heads, head_dim)
        values = all_kv[:, :, width:].reshape(items, full_dec, heads, head_dim)
        attended, self_lse = attend_forward(query, keys, values, self_attention_bias, self_mask)
        attended = attended.reshape(-1, width)
        after_self = inputs + matmul(attended, wso)
        normed_two = rms_norm(after_self, norm_gains[1]).astype(jnp.bfloat16)
        local_cq = matmul(normed_two, wcq).astype(jnp.bfloat16)
        local_ckv = matmul(enc_rows, wckv).astype(jnp.bfloat16).reshape(items, local_enc, 2 * width)
        cross_query = local_cq.reshape(items, local_dec, heads, head_dim)
        all_ckv = lax.all_gather(local_ckv, "seq", axis=1, tiled=True)
        cross_keys = all_ckv[:, :, :width].reshape(items, full_enc, heads, head_dim)
        cross_values = all_ckv[:, :, width:].reshape(items, full_enc, heads, head_dim)
        cross_att, cross_lse = attend_forward(
            cross_query, cross_keys, cross_values, 0.0, cross_mask
        )
        cross_att = cross_att.reshape(-1, width)
        after_cross = after_self + matmul(cross_att, wco)
        normed_three = rms_norm(after_cross, norm_gains[2]).astype(jnp.bfloat16)
        pre = matmul(normed_three, win)
        act = smooth_gelu(pre).astype(jnp.bfloat16)
        result = after_cross + matmul(act, wout)
        return dict(
            normed=normed,
            qkv=qkv,
            query=query,
            keys=keys,
            values=values,
            attended=attended,
            self_lse=self_lse,
            after_self=after_self,
            normed_two=normed_two,
            cross_query=cross_query,
            cross_keys=cross_keys,
            cross_values=cross_values,
            cross_att=cross_att,
            cross_lse=cross_lse,
            cross_part_mask=cross_mask,
            after_cross=after_cross,
            normed_three=normed_three,
            pre=pre,
            act=act,
            result=result,
        )

    shards = (w_self_qkv, w_self_out, w_cross_q, w_cross_kv, w_cross_out, w_ffn_in, w_ffn_out)
    first = (
        lax.all_gather(shards[0], ("dp", "seq"), axis=0, tiled=True),
        lax.all_gather(shards[1], ("dp", "seq"), axis=0, tiled=True),
        lax.all_gather(shards[2], ("dp", "seq"), axis=0, tiled=True),
        lax.all_gather(shards[3], ("dp", "seq"), axis=0, tiled=True),
        lax.all_gather(shards[4], ("dp", "seq"), axis=0, tiled=True),
        lax.all_gather(shards[5], ("dp", "seq"), axis=0, tiled=True),
        lax.all_gather(shards[6], ("dp", "seq"), axis=0, tiled=True),
    )
    state = forward_pass(first)
    output = state["result"]
    weights = first
    weights = (
        lax.all_gather(shards[0], ("dp", "seq"), axis=0, tiled=True),
        lax.all_gather(shards[1], ("dp", "seq"), axis=0, tiled=True),
        lax.all_gather(shards[2], ("dp", "seq"), axis=0, tiled=True),
        lax.all_gather(shards[3], ("dp", "seq"), axis=0, tiled=True),
        lax.all_gather(shards[4], ("dp", "seq"), axis=0, tiled=True),
        lax.all_gather(shards[5], ("dp", "seq"), axis=0, tiled=True),
        lax.all_gather(shards[6], ("dp", "seq"), axis=0, tiled=True),
    )
    state = forward_pass(weights)
    wqkv, wso, wcq, wckv, wco, win, wout = weights
    grad_top = cotangent.reshape(-1, width).astype(jnp.float32)
    grad_low = grad_top.astype(jnp.bfloat16)
    grad_wout = contract_rows(state["act"], grad_low)
    grad_act = contract_cols(grad_low, wout)
    grad_pre = jax.vjp(smooth_gelu, state["pre"])[1](grad_act)[0].astype(jnp.bfloat16)
    grad_win = contract_rows(state["normed_three"], grad_pre)
    normalized_gradient = contract_cols(grad_pre, win)
    norm_back, gain_three = jax.vjp(rms_norm, state["after_cross"], norm_gains[2])[1](
        normalized_gradient
    )
    cross_attention_gradient = grad_top + norm_back
    cross_low = cross_attention_gradient.astype(jnp.bfloat16)
    grad_wco = contract_rows(state["cross_att"], cross_low)
    grad_catt_local = contract_cols(cross_low, wco).astype(jnp.bfloat16)
    grad_catt = grad_catt_local.reshape(items, local_dec, heads, head_dim)
    grad_cq, grad_ck, grad_cv, unused_scores = attend_backward(
        state["cross_query"],
        state["cross_keys"],
        state["cross_values"],
        0.0,
        cross_mask,
        state["cross_lse"],
        grad_catt,
    )
    grad_ckv_terms = jnp.concatenate(
        [grad_ck.reshape(items, full_enc, width), grad_cv.reshape(items, full_enc, width)], axis=-1
    )
    grad_ckv = lax.psum_scatter(
        grad_ckv_terms.astype(jnp.bfloat16), "seq", scatter_dimension=1, tiled=True
    ).reshape(-1, 2 * width)
    grad_cq_low = grad_cq.reshape(-1, width).astype(jnp.bfloat16)
    grad_wckv = contract_rows(enc_rows, grad_ckv)
    grad_enc = contract_cols(grad_ckv, wckv).astype(jnp.bfloat16).reshape(encoded.shape)
    grad_wcq = contract_rows(state["normed_two"], grad_cq_low)
    second_normalized_gradient = contract_cols(grad_cq_low, wcq)
    norm_back_two, gain_two = jax.vjp(rms_norm, state["after_self"], norm_gains[1])[1](
        second_normalized_gradient
    )
    grad_self = cross_attention_gradient + norm_back_two
    self_low = grad_self.astype(jnp.bfloat16)
    grad_wso = contract_rows(state["attended"], self_low)
    grad_att = (
        contract_cols(self_low, wso).astype(jnp.bfloat16).reshape(items, local_dec, heads, head_dim)
    )
    grad_q, grad_k, grad_v, grad_scores = attend_backward(
        state["query"],
        state["keys"],
        state["values"],
        self_attention_bias,
        self_mask,
        state["self_lse"],
        grad_att,
    )
    score_totals = jnp.sum(grad_scores.astype(jnp.float32), axis=0)
    bias_gradient = jnp.einsum(
        "xru,pru->xp", bucket_indicator, score_totals, precision=lax.Precision.HIGHEST
    )
    grad_kv_terms = jnp.concatenate(
        [grad_k.reshape(items, full_dec, width), grad_v.reshape(items, full_dec, width)], axis=-1
    )
    grad_kv = lax.psum_scatter(
        grad_kv_terms.astype(jnp.bfloat16), "seq", scatter_dimension=1, tiled=True
    ).reshape(-1, 2 * width)
    grad_qkv = jnp.concatenate([grad_q.reshape(-1, width).astype(jnp.bfloat16), grad_kv], axis=-1)
    grad_wqkv = contract_rows(state["normed"], grad_qkv)
    grad_normed_one = contract_cols(grad_qkv, wqkv)
    norm_back_one, gain_one = jax.vjp(rms_norm, inputs, norm_gains[0])[1](grad_normed_one)
    grad_inputs = (grad_self + norm_back_one).astype(jnp.bfloat16).reshape(hidden.shape)
    full_terms = (grad_wqkv, grad_wso, grad_wcq, grad_wckv, grad_wco, grad_win, grad_wout)
    tiled = tuple((term.reshape(8 * device_count, -1) for term in full_terms))
    summed = (
        lax.psum_scatter(tiled[0], ("dp", "seq"), scatter_dimension=0, tiled=True),
        lax.psum_scatter(tiled[1], ("dp", "seq"), scatter_dimension=0, tiled=True),
        lax.psum_scatter(tiled[2], ("dp", "seq"), scatter_dimension=0, tiled=True),
        lax.psum_scatter(tiled[3], ("dp", "seq"), scatter_dimension=0, tiled=True),
        lax.psum_scatter(tiled[4], ("dp", "seq"), scatter_dimension=0, tiled=True),
        lax.psum_scatter(tiled[5], ("dp", "seq"), scatter_dimension=0, tiled=True),
        lax.psum_scatter(tiled[6], ("dp", "seq"), scatter_dimension=0, tiled=True),
    )
    summed = tuple((piece.reshape(-1, term.shape[1]) for piece, term in zip(summed, full_terms)))
    gain_grads, table_grads = lax.psum(
        (jnp.stack([gain_one, gain_two, gain_three]), bias_gradient), ("dp", "seq")
    )
    block_out = output.astype(jnp.bfloat16).reshape(hidden.shape)
    return (
        block_out,
        grad_inputs,
        grad_enc,
        summed[0],
        summed[1],
        summed[2],
        summed[3],
        summed[4],
        summed[5],
        summed[6],
        gain_grads,
        table_grads,
    )


pair = 128


def nt(left, right):
    return lax.dot_general(left, right, (((1,), (1,)), ((), ())), preferred_element_type=jnp.float32)


masked_bucket = pair - 1


def half_masks():
    lane = lax.broadcasted_iota(jnp.int32, (1, pair), 1)
    low = (lane < pair // 2).astype(jnp.float32).astype(jnp.bfloat16)
    high = (lane >= pair // 2).astype(jnp.float32).astype(jnp.bfloat16)
    return (low, high)


def look_up(row, ids):
    spread = jnp.broadcast_to(row, (ids.shape[0], pair))
    pieces = [
        jnp.take_along_axis(spread, ids[:, at : at + pair], axis=1, mode="promise_in_bounds")
        for at in range(0, ids.shape[1], pair)
    ]
    return jnp.concatenate(pieces, axis=1)


def store_lse(lse_ref, columns):
    lane = lax.broadcasted_iota(jnp.int32, (columns[0].shape[0], pair), 1)
    both = jnp.where(lane == 0, columns[0], columns[1])
    lse_ref[...] = jnp.transpose(both)[: lse_ref.shape[0]]


def attend_rows(scores, values):
    top = jnp.max(scores, axis=1, keepdims=True)
    expo = jnp.exp(scores - top)
    total = jnp.sum(expo, axis=1, keepdims=True)
    output = matmul(expo.astype(jnp.bfloat16), values)
    return output / total, top + jnp.log(total)


def self_forward_kernel(q_ref, k_ref, v_ref, ids_ref, table_ref, att_ref, full_ref, lse_ref, *, block):
    rows = q_ref.shape[0]
    low, high = half_masks()
    lane = lax.broadcasted_iota(jnp.int32, (block, pair), 1)
    columns = ([], [])
    for start in range(0, rows, block):
        span = start + block
        here = slice(start, span)
        query = q_ref[here, :] * jnp.bfloat16(score_scale)
        outs = []
        for side, mask in enumerate((low, high)):
            scores = nt(query * mask, k_ref[:span, :])
            scores = scores + look_up(table_ref[0, side : side + 1, :], ids_ref[here, :span])
            output, lse = attend_rows(scores, v_ref[:span, :])
            outs.append(output)
            columns[side].append(lse)
        both = jnp.where(lane < pair // 2, outs[0], outs[1])
        full_ref[here, :] = both
        att_ref[here, :] = both.astype(jnp.bfloat16)
    store_lse(lse_ref, [jnp.concatenate(column, axis=0) for column in columns])


def cross_forward_kernel(q_ref, k_ref, v_ref, tag_ref, mark_ref, att_ref, full_ref, lse_ref, *, block):
    rows = q_ref.shape[0]
    low, high = half_masks()
    lane = lax.broadcasted_iota(jnp.int32, (block, pair), 1)
    keys = [k_ref[...] * mask + mark_ref[...] * other for mask, other in ((low, high), (high, low))]
    columns = ([], [])
    for start in range(0, rows, block):
        here = slice(start, start + block)
        query = q_ref[here, :] * jnp.bfloat16(score_scale)
        outs = []
        for side, (mask, other) in enumerate(((low, high), (high, low))):
            scores = nt(query * mask + tag_ref[here, :] * other, keys[side])
            output, lse = attend_rows(scores, v_ref[...])
            outs.append(output)
            columns[side].append(lse)
        both = jnp.where(lane < pair // 2, outs[0], outs[1])
        full_ref[here, :] = both
        att_ref[here, :] = both.astype(jnp.bfloat16)
    store_lse(lse_ref, [jnp.concatenate(column, axis=0) for column in columns])


def inner_rows(grad_ref, full_ref):
    product = jnp.transpose(grad_ref[...].astype(jnp.float32) * full_ref[...])
    half = pair // 2
    return [jnp.sum(product[at : at + half], axis=0, keepdims=True) for at in (0, half)]


def backward_chunk(key, key_t, value, query, query_ext, grad, lse, inner, bias):
    scores = nt(key, query_ext)
    if bias is not None:
        scores = scores + bias
    probs = jnp.exp(scores - lse)
    grad_probs = nt(value, grad)
    grad_scores = (probs * (grad_probs - inner)).astype(jnp.bfloat16)
    grad_value = matmul(probs.astype(jnp.bfloat16), grad)
    grad_key = matmul(grad_scores, query)
    grad_query_t = matmul(key_t, grad_scores)
    return grad_scores, grad_value, grad_key, grad_query_t


def rms_rows(values, gain):
    scale = lax.rsqrt(jnp.mean(values * values, axis=1, keepdims=True) + epsilon)
    return (values * scale * gain).astype(jnp.bfloat16)


class Given(typing.NamedTuple):
    length: typing.Any
    ids: typing.Any
    tag: typing.Any
    mark: typing.Any
    table: typing.Any
    gains: typing.Any
    x: typing.Any
    wqkv: typing.Any


class Fetched(typing.NamedTuple):
    enc: typing.Any
    wso: typing.Any
    wcq: typing.Any
    wckv: typing.Any
    wco: typing.Any


class Kept(typing.NamedTuple):
    n1: typing.Any
    ids_t: typing.Any
    qkv: typing.Any
    att: typing.Any
    sfull: typing.Any
    x1: typing.Any
    n2: typing.Any
    cq: typing.Any
    ckv: typing.Any
    catt: typing.Any
    cfull: typing.Any
    x2: typing.Any
    n3: typing.Any


def attention_forward_kernel(*refs, pairs, block):
    refs = list(refs)

    def take(kind):
        taken = kind(*refs[: len(kind._fields)])
        del refs[: len(kind._fields)]
        return taken

    given, distant, kept = take(Given), take(Fetched), take(Kept)
    slse_ref, clse_ref = refs[:2]
    del refs[:2]
    here, near = take(Kept), take(Fetched)
    masked, fetch_sem, keep_sem = refs
    made, wanted = Kept(*range(len(here))), Fetched(*range(len(near)))
    at = pl.program_id(0)
    rows, width = here.att.shape

    def lanes(index):
        return pl.ds(pl.multiple_of(index * pair, pair), pair)

    def columns(panel):
        return slice(panel * width, (panel + 1) * width)

    def fetch(i):
        return pltpu.make_async_copy(distant[i], near[i], fetch_sem.at[i])

    def ship(i):
        return pltpu.make_async_copy(here[i], kept[i], keep_sem.at[i])

    @pl.when(at == 0)
    def _():
        for i in wanted:
            fetch(i).start()
        gain = given.gains[0:1, :]
        for start in range(0, rows, block):
            rest = slice(start, start + block)
            here.n1[rest, :] = rms_rows(given.x[rest, :].astype(jnp.float32), gain)
            for wide in range(0, rows, block):
                query = lax.broadcasted_iota(jnp.int32, (block, block), 0) + start
                key = lax.broadcasted_iota(jnp.int32, (block, block), 1) + wide
                keep = (key <= query) & (key < given.length[0:1, :])
                ids = given.ids[rest, wide : wide + block].astype(jnp.float32)
                ids = jnp.where(keep, ids, float(masked_bucket))
                masked[rest, wide : wide + block] = ids.astype(jnp.int32)
                here.ids_t[wide : wide + block, rest] = jnp.transpose(ids).astype(jnp.int32)
        ship(made.n1).start()
        ship(made.ids_t).start()

    @pl.when(at == 1)
    def _():
        for panel in range(3):
            product_rows(here.n1, given.wqkv.at[:, columns(panel)], here.qkv.at[:, columns(panel)], 2 * block)
        ship(made.qkv).start()

    @pl.when((at > 1) & (at <= pairs + 1))
    def _():
        index = at - 2
        self_forward_kernel(
            here.qkv.at[:, lanes(index)],
            here.qkv.at[:, lanes(pairs + index)],
            here.qkv.at[:, lanes(2 * pairs + index)],
            masked,
            given.table.at[pl.ds(index, 1)],
            here.att.at[:, lanes(index)],
            here.sfull.at[:, lanes(index)],
            slse_ref,
            block=block,
        )

    @pl.when(at == pairs + 2)
    def _():
        fetch(wanted.wso).wait()
        fetch(wanted.wcq).wait()
        for start in range(0, rows, 2 * block):
            rest = slice(start, start + 2 * block)
            total = given.x[rest, :].astype(jnp.float32) + matmul(here.att[rest, :], near.wso[...])
            here.x1[rest, :] = total
            here.n2[rest, :] = rms_rows(total, given.gains[1:2, :])
        product_rows(here.n2, near.wcq, here.cq, 2 * block)
        for i in (made.att, made.sfull, made.x1, made.n2, made.cq):
            ship(i).start()

    @pl.when(at == pairs + 3)
    def _():
        fetch(wanted.enc).wait()
        fetch(wanted.wckv).wait()
        for panel in range(2):
            product_rows(near.enc, near.wckv.at[:, columns(panel)], here.ckv.at[:, columns(panel)], 2 * block)
        ship(made.ckv).start()

    @pl.when((at > pairs + 3) & (at <= 2 * pairs + 3))
    def _():
        index = at - pairs - 4
        cross_forward_kernel(
            here.cq.at[:, lanes(index)],
            here.ckv.at[:, lanes(index)],
            here.ckv.at[:, lanes(pairs + index)],
            given.tag,
            given.mark,
            here.catt.at[:, lanes(index)],
            here.cfull.at[:, lanes(index)],
            clse_ref,
            block=block,
        )

    @pl.when(at == 2 * pairs + 4)
    def _():
        ship(made.catt).start()
        ship(made.cfull).start()
        fetch(wanted.wco).wait()
        for start in range(0, rows, 2 * block):
            rest = slice(start, start + 2 * block)
            total = here.x1[rest, :] + matmul(here.catt[rest, :], near.wco[...])
            here.x2[rest, :] = total
            here.n3[rest, :] = rms_rows(total, given.gains[2:3, :])
        ship(made.x2).start()
        ship(made.n3).start()
        for i in made:
            ship(i).wait()


def cross_backward_pair(q_ref, k_ref, v_ref, tag_ref, mark_ref, grad_ref, full_ref, lse_ref, query_t, *, block, put):
    low, high = half_masks()
    inner = inner_rows(grad_ref, full_ref)
    query = q_ref[...] * jnp.bfloat16(score_scale)
    queries = [query * low, query * high]
    exts = [queries[0] + tag_ref[...] * high, queries[1] + tag_ref[...] * low]
    grads = [grad_ref[...] * low, grad_ref[...] * high]
    for start in range(0, k_ref.shape[0], block):
        here = slice(start, start + block)
        key = k_ref[here, :]
        parts = [None, None, None]
        for side, (mask, other) in enumerate(((low, high), (high, low))):
            own = key * mask
            _, *news = backward_chunk(
                own + mark_ref[here, :] * other,
                jnp.transpose(own),
                v_ref[here, :],
                queries[side],
                exts[side],
                grads[side],
                lse_ref[side : side + 1, :],
                inner[side],
                None,
            )
            parts = [new if part is None else part + new for part, new in zip(parts, news)]
        put(2, here, parts[0].astype(jnp.bfloat16))
        put(1, here, parts[1].astype(jnp.bfloat16))
        query_t[...] = parts[2] if start == 0 else query_t[...] + parts[2]
    put(0, slice(None), (jnp.transpose(query_t[...]) * score_scale).astype(jnp.bfloat16))


def self_backward_pair(q_ref, k_ref, v_ref, ids_ref, table_ref, grad_ref, full_ref, lse_ref, ds_ref, query_t, *, block, put):
    low, high = half_masks()
    inner = inner_rows(grad_ref, full_ref)
    query = q_ref[...] * jnp.bfloat16(score_scale)
    for start in range(0, k_ref.shape[0], block):
        here = slice(start, start + block)
        key = k_ref[here, :]
        parts = [None, None, None]
        for side, mask in enumerate((low, high)):
            own = query[start:, :] * mask
            scores, *news = backward_chunk(
                key,
                jnp.transpose(key * mask),
                v_ref[here, :],
                own,
                own,
                grad_ref[start:, :] * mask,
                lse_ref[side : side + 1, start:],
                inner[side][:, start:],
                look_up(table_ref[0, side : side + 1, :], ids_ref[here, start:]),
            )
            ds_ref[side, here, start:] = scores
            parts = [new if part is None else part + new for part, new in zip(parts, news)]
        put(2, here, parts[0].astype(jnp.bfloat16))
        put(1, here, parts[1].astype(jnp.bfloat16))
        if start == 0:
            query_t[...] = parts[2]
        else:
            query_t[:, start:] += parts[2]
    put(0, slice(None), (jnp.transpose(query_t[...]) * score_scale).astype(jnp.bfloat16))


def rms_back_rows(values, gain, grad):
    scale = lax.rsqrt(jnp.mean(values * values, axis=1, keepdims=True) + epsilon)
    weighted = grad * gain
    inner = jnp.mean(values * weighted, axis=1, keepdims=True)
    back = scale * weighted - values * (scale * scale * scale * inner)
    return back, jnp.sum(grad * values * scale, axis=0, keepdims=True)


def turn(source, target):
    rows, columns = source.shape
    for start in range(0, columns, pair):
        target[start : start + pair, :rows] = jnp.transpose(source[:, start : start + pair])


def product_rows(left, right, target, block, dims=(((1,), (0,)), ((), ()))):
    for start in range(0, target.shape[0], block):
        here = slice(start, start + block)
        product = lax.dot_general(left[here, :], right[...], dims, preferred_element_type=jnp.float32)
        target[here, :] = product.astype(jnp.bfloat16)


nt_dims = (((1,), (1,)), ((), ()))


def attention_backward_kernel(
    cq_ref,
    ck_ref,
    cv_ref,
    tag_ref,
    mark_ref,
    gcatt_ref,
    cfull_ref,
    clse_ref,
    q_ref,
    k_ref,
    v_ref,
    ids_ref,
    table_ref,
    sfull_ref,
    slse_ref,
    gains_ref,
    x_ref,
    x1_ref,
    gx2_ref,
    n1_ref,
    n2_ref,
    att_ref,
    enc_ref,
    wcq_ref,
    wso_ref,
    wckv_ref,
    wqkv_ref,
    ds_ref,
    gwqkv_ref,
    gwckv_ref,
    gwcq_ref,
    gwso_ref,
    enc_items,
    x_items,
    ggain_ref,
    gcq,
    gckv,
    gqkv,
    gx1,
    low_x1,
    gatt,
    total,
    tall,
    query_t,
    genc,
    gx,
    *swap_sems,
    pairs,
    block,
):
    enc_sems, x_sems = swap_sems[:3], swap_sems[3:]
    at = pl.program_id(0)
    rows, width = gcq.shape
    keys = gckv.shape[0]

    def lanes(first, index):
        return pl.ds(pl.multiple_of(first + index * pair, pair), pair)

    @pl.when(at < pairs)
    def _():
        def put(kind, where, values):
            if kind == 0:
                gcq[where, lanes(0, at)] = values
            else:
                gckv[where, lanes((kind - 1) * width, at)] = values

        cross_backward_pair(
            cq_ref, ck_ref, cv_ref, tag_ref, mark_ref, gcatt_ref, cfull_ref, clse_ref, query_t, block=2 * block, put=put
        )

    @pl.when(at == pairs)
    def _():
        gain = gains_ref[1:2, :]
        sums = None
        for start in range(0, rows, block):
            here = slice(start, start + block)
            back, part = rms_back_rows(x1_ref[here, :], gain, nt(gcq[here, :], wcq_ref[...]))
            gx1[here, :] = gx2_ref[here, :] + back
            low_x1[here, :] = gx1[here, :].astype(jnp.bfloat16)
            sums = part if sums is None else sums + part
        ggain_ref[1:2, :] = sums
        product_rows(low_x1, wso_ref, gatt, 2 * block, nt_dims)

    enc_pieces, x_pieces = enc_sems[1].shape[0], x_sems[1].shape[0]
    enc_swap = LateSwap(genc, enc_items, enc_sems, enc_pieces)
    x_swap = LateSwap(gx, x_items, x_sems, x_pieces)

    @pl.when(at == pairs + 1)
    def _():
        product_rows(gckv, wckv_ref, genc, 2 * block, nt_dims)

    for piece in range(enc_pieces):
        pl.when(at == min(pairs + 2 + piece, 2 * pairs + 5))(functools.partial(enc_swap.begin, piece))

    @pl.when((at > pairs + 1) & (at <= 2 * pairs + 1))
    def _():
        index = at - pairs - 2

        def put(kind, where, values):
            gqkv[where, lanes(kind * width, index)] = values

        self_backward_pair(
            q_ref,
            k_ref,
            v_ref,
            ids_ref,
            table_ref,
            gatt.at[:, lanes(0, index)],
            sfull_ref,
            slse_ref,
            ds_ref,
            query_t,
            block=block,
            put=put,
        )

    @pl.when(at == 2 * pairs + 2)
    def _():
        turn(n1_ref, tall)

    for panel in range(3):

        @pl.when(at == 2 * pairs + 2 + panel)
        def _(panel=panel):
            columns = slice(panel * width, (panel + 1) * width)
            product_rows(tall.at[:, :rows], gqkv.at[:, columns], gwqkv_ref, 2 * block)
            for start in range(0, rows, 2 * block):
                here = slice(start, start + 2 * block)
                part = nt(gqkv[here, columns], wqkv_ref[...])
                total[here, :] = part if panel == 0 else total[here, :] + part

    @pl.when(at == 2 * pairs + 4)
    def _():
        gain = gains_ref[0:1, :]
        sums = None
        for start in range(0, rows, block):
            here = slice(start, start + block)
            back, part = rms_back_rows(x_ref[here, :].astype(jnp.float32), gain, total[here, :])
            gx[here, :] = (gx1[here, :] + back).astype(jnp.bfloat16)
            sums = part if sums is None else sums + part
        ggain_ref[0:1, :] = sums
        for piece in range(x_pieces):
            x_swap.begin(piece)

    @pl.when(at == 2 * pairs + 5)
    def _():
        turn(enc_ref, tall)
        for panel in range(2):
            columns = slice(panel * width, (panel + 1) * width)
            product_rows(tall.at[:, :keys], gckv.at[:, columns], gwckv_ref.at[:, columns], 2 * block)

    @pl.when(at == 2 * pairs + 6)
    def _():
        turn(n2_ref, tall)
        product_rows(tall.at[:, :rows], gcq, gwcq_ref, 2 * block)
        turn(att_ref, tall)
        product_rows(tall.at[:, :rows], low_x1, gwso_ref, 2 * block)
        enc_swap.finish()
        x_swap.finish()


def table_kernel(gains_ref, ids_ref, ds_ref, out_ref, sums, spread, table, total, came, send, recv, *, buckets):
    heads, block = ds_ref.shape[0], ds_ref.shape[1]

    @pl.when(pl.program_id(0) == 0)
    def _():
        sums[...] = jnp.zeros_like(sums)

    spread[...] = ds_ref[...].astype(jnp.float32)
    ids = ids_ref[...]

    def step(bucket, carry):
        chosen = ids == bucket
        for head in range(heads):
            picked = jnp.where(chosen, spread[head], 0.0).reshape(block // 8, 8, pair)
            sums[bucket, head] += jnp.sum(picked, axis=0)
        return carry

    lax.fori_loop(0, buckets, step, 0)


def table_finish(gains_ref, ids_ref, ds_ref, out_ref, sums, spread, table, total, came, send, recv):
    heads = ds_ref.shape[0]

    def fill():
        table[...] = jnp.zeros_like(table)
        table[:, :heads] = jnp.sum(jnp.sum(sums[...], axis=3), axis=2)
        total[0] = jnp.concatenate([gains_ref[...], table[...]], axis=0)

    def finish():
        out_ref[...] = total[4]

    return reduce_steps(fill, total, came, send, recv, finish)


def block_of(rows, first=0):
    return pl.BlockSpec((rows, pair), lambda at: (0, first + at))


def whole(shape):
    return pl.BlockSpec(shape, lambda at: (0,) * len(shape))


def attention_forward(length, ids, tag_lanes, mark_lanes, table, gains, states, wqkv, enc, wso, wcq, wckv, wco, moves):
    rows, width = states.shape
    keys = enc.shape[0]
    pairs = width // pair
    low, high = jnp.bfloat16, jnp.float32
    shapes = Kept(
        n1=((rows, width), low),
        ids_t=((rows, rows), jnp.int32),
        qkv=((rows, 3 * width), low),
        att=((rows, width), low),
        sfull=((rows, width), high),
        x1=((rows, width), high),
        n2=((rows, width), low),
        cq=((rows, width), low),
        ckv=((keys, 2 * width), low),
        catt=((rows, width), low),
        cfull=((rows, width), high),
        x2=((rows, width), high),
        n3=((rows, width), low),
    )

    def once(values):
        return pl.BlockSpec(values.shape, lambda at: (0,) * len(values.shape), pipeline_mode=pl.Buffered(1))

    anywhere = pl.BlockSpec(memory_space=pl.ANY)
    given = (length, ids, tag_lanes, mark_lanes, table, gains, states, wqkv)
    distant = (enc, wso, wcq, wckv, wco)
    outs, moved = carried(
        functools.partial(attention_forward_kernel, pairs=pairs, block=128),
        moves,
        grid=(2 * pairs + 5,),
        in_specs=[*(once(values) for values in given), *(anywhere for _ in distant)],
        out_specs=[anywhere] * len(shapes)
        + [
            pl.BlockSpec((8, rows), lambda at: (jnp.clip(at - 2, 0, pairs - 1), 0)),
            pl.BlockSpec((8, rows), lambda at: (jnp.clip(at - pairs - 4, 0, pairs - 1), 0)),
        ],
        out_shape=[jax.ShapeDtypeStruct(*shape) for shape in shapes]
        + [jax.ShapeDtypeStruct((pairs * 8, rows), high)] * 2,
        scratch_shapes=[pltpu.VMEM(*shape) for shape in shapes]
        + [pltpu.VMEM(values.shape, values.dtype) for values in distant]
        + [
            pltpu.VMEM((rows, rows), jnp.int32),
            pltpu.SemaphoreType.DMA((len(distant),)),
            pltpu.SemaphoreType.DMA((len(shapes),)),
        ],
        ident=1,
        name="attention_forward",
        tail=2,
    )(*given, *distant)
    return Kept(*outs[: len(shapes)]), outs[len(shapes) :], moved


def deliver_kernel(*refs):
    count = len(refs) // 3
    sems = refs[-1]
    incoming = [pltpu.make_async_copy(refs[i], refs[2 * count + i], sems.at[i]) for i in range(count)]
    outgoing = [pltpu.make_async_copy(refs[2 * count + i], refs[count + i], sems.at[i]) for i in range(count)]
    for copy in incoming:
        copy.start()
    for one, other in zip(incoming, outgoing):
        one.wait()
        other.start()
    for copy in outgoing:
        copy.wait()


def deliver(results):
    anywhere = pl.BlockSpec(memory_space=pl.ANY)
    return pl.pallas_call(
        deliver_kernel,
        in_specs=[anywhere] * len(results),
        out_specs=[anywhere] * len(results),
        out_shape=[jax.ShapeDtypeStruct(result.shape, result.dtype) for result in results],
        scratch_shapes=[pltpu.VMEM(result.shape, result.dtype) for result in results]
        + [pltpu.SemaphoreType.DMA((len(results),))],
        compiler_params=pltpu.CompilerParams(vmem_limit_bytes=32 * 1024 * 1024),
        name="deliver",
    )(*results)


def attention_backward(
    query, ckv, tag_lanes, mark_lanes, grad_catt, cross_full, cross_lse,
    qkv, ids_t, table, self_full, self_lse,
    gains, states, after_self, grad_cross, normed, normed_two, attended, enc_rows,
    wcq, wso, wckv, wqkv, moves,
):
    rows, width = query.shape
    keys = ckv.shape[0]
    pairs = width // pair
    last = pairs - 1

    def cross_block(count, first=0):
        return pl.BlockSpec((count, pair), lambda at: (0, first + jnp.minimum(at, last)))

    def self_index(at):
        return jnp.clip(at - pairs - 2, 0, last)

    def self_block(count, first=0):
        return pl.BlockSpec((count, pair), lambda at: (0, first + self_index(at)))

    def once(values):
        return pl.BlockSpec(values.shape, lambda at: (0,) * len(values.shape), pipeline_mode=pl.Buffered(1))

    def panel(count):
        return pl.BlockSpec((count, width), lambda at: (0, jnp.clip(at - 2 * pairs - 2, 0, 2)))

    low = jnp.bfloat16
    wholes = [(width, 2 * width), (width, width), (width, width)]
    items = [(2, keys // 2, width), (2, rows // 2, width)]
    return carried(
        functools.partial(attention_backward_kernel, pairs=pairs, block=128),
        moves,
        grid=(2 * pairs + 7,),
        in_specs=[
            cross_block(rows),
            cross_block(keys),
            cross_block(keys, pairs),
            once(tag_lanes),
            once(mark_lanes),
            cross_block(rows),
            cross_block(rows),
            pl.BlockSpec((8, rows), lambda at: (jnp.minimum(at, last), 0)),
            self_block(rows),
            self_block(rows, pairs),
            self_block(rows, 2 * pairs),
            once(ids_t),
            pl.BlockSpec((1, 2, pair), lambda at: (self_index(at), 0, 0)),
            self_block(rows),
            pl.BlockSpec((8, rows), lambda at: (self_index(at), 0)),
            *(
                once(values)
                for values in (gains, states, after_self, grad_cross, normed, normed_two, attended, enc_rows, wcq, wso, wckv)
            ),
            panel(width),
        ],
        out_specs=[
            pl.BlockSpec((2, rows, rows), lambda at: (self_index(at), 0, 0)),
            panel(width),
            *(pl.BlockSpec(shape, lambda at: (0, 0), pipeline_mode=pl.Buffered(1)) for shape in wholes),
            *(pl.BlockSpec(memory_space=pl.ANY) for _ in items),
            pl.BlockSpec((8, width), lambda at: (0, 0)),
        ],
        out_shape=[
            jax.ShapeDtypeStruct((pairs * 2, rows, rows), low),
            jax.ShapeDtypeStruct((width, 3 * width), low),
            *(jax.ShapeDtypeStruct(shape, low) for shape in wholes + items),
            jax.ShapeDtypeStruct((8, width), jnp.float32),
        ],
        scratch_shapes=[
            pltpu.VMEM((rows, width), low),
            pltpu.VMEM((keys, 2 * width), low),
            pltpu.VMEM((rows, 3 * width), low),
            pltpu.VMEM((rows, width), jnp.float32),
            pltpu.VMEM((rows, width), low),
            pltpu.VMEM((rows, width), low),
            pltpu.VMEM((rows, width), jnp.float32),
            pltpu.VMEM((width, keys), low),
            pltpu.VMEM((pair, rows), jnp.float32),
            pltpu.VMEM((keys, width), low),
            pltpu.VMEM((rows, width), low),
            *(pltpu.SemaphoreType.DMA((count,)) for count in (1, 8, 8, 1, 2, 2)),
        ],
        ident=3,
        name="attention_backward",
        tail=0,
    )(
        query, ckv, ckv, tag_lanes, mark_lanes, grad_catt, cross_full, cross_lse,
        qkv, qkv, qkv, ids_t, table, self_full, self_lse,
        gains, states, after_self, grad_cross, normed, normed_two, attended, enc_rows,
        wcq, wso, wckv, wqkv,
    )


def table_sums(gains, ids_t, grad_scores, buckets, moves):
    heads = grad_scores.shape[0]
    side = ids_t.shape[0] // pair
    starts = [sum(side - row for row in range(before)) for before in range(1, side)]

    def place(at):
        row, column = 0, at
        for back, start in enumerate(starts):
            past = jnp.where(at >= start, 1, 0)
            row = row + past
            column = column - past * (side - 1 - back)
        return row, column

    small = (gains.shape[0] + buckets, pair)
    return carried(
        functools.partial(table_kernel, buckets=buckets),
        moves,
        grid=(side * (side + 1) // 2,),
        in_specs=[
            whole(gains.shape),
            pl.BlockSpec((pair, pair), place),
            pl.BlockSpec((heads, pair, pair), lambda at: (0, *place(at))),
        ],
        out_specs=[whole(small)],
        out_shape=[jax.ShapeDtypeStruct(small, jnp.float32)],
        scratch_shapes=[
            pltpu.VMEM((buckets, heads, 8, pair), jnp.float32),
            pltpu.VMEM((heads, pair, pair), jnp.float32),
            pltpu.VMEM((buckets, pair), jnp.float32),
            pltpu.VMEM((5,) + small, jnp.float32),
            pltpu.VMEM((6,) + small, jnp.float32),
            pltpu.SemaphoreType.DMA((6,)),
            pltpu.SemaphoreType.DMA((6,)),
        ],
        ident=5,
        name="table_sums",
        last=table_finish,
        tail=9,
    )(gains, ids_t, grad_scores)


def bring(moves):
    return carried(
        None, moves, grid=(1,), in_specs=[], out_specs=[], out_shape=[], scratch_shapes=[], ident=0, name="bring"
    )()[1]


MESH = pl.DeviceIdType.MESH
grid_z, grid_x, grid_core, grid_y = 4, 2, 2, 2
kept_slots = 3
lag = 2
swap_rows = 128
block_grid = (grid_z, grid_x, grid_core, grid_y)


def position():
    at = lax.axis_index("dp")
    return at // 4, (at // 2) % 2, at % 2, lax.axis_index("seq")


def device_at(z, x, core, y):
    return ((z * grid_x + x) * grid_core + core, y)


def partners():
    z, x, core, y = position()
    along = [device_at((z + step) % grid_z, x, core, y) for step in range(1, grid_z)]
    return along + [device_at(z, 1 - x, core, y), device_at(z, x, core, 1 - y), device_at(z, x, 1 - core, y)]


def meet():
    barrier = pltpu.get_barrier_semaphore()
    others = partners()
    for other in others:
        pl.semaphore_signal(barrier, inc=1, device_id=other, device_id_type=MESH)
    pl.semaphore_wait(barrier, len(others))


def remote(source, target, send, recv, other):
    return pltpu.make_async_remote_copy(
        src_ref=source, dst_ref=target, send_sem=send, recv_sem=recv, device_id=other, device_id_type=MESH
    )


def each(sizes, body):
    total = 1
    for size in sizes:
        total *= size

    def step(at, carry):
        indices = []
        for size in reversed(sizes):
            indices.append(at % size)
            at = at // size
        body(*reversed(indices))
        return carry

    lax.fori_loop(0, total, step, 0)


def pieces_of(rows):
    size = min(rows, swap_rows)
    return [(start, size) for start in range(0, rows, size)]


def swap_steps(halves, outs, items, sems):
    local, send, recv = sems
    y = position()[3]
    across_y = partners()[4]
    pieces = [(i, *piece) for i, half in enumerate(halves) for piece in pieces_of(half.shape[1])]

    def crossing(at):
        i, start, size = pieces[at]
        rows = pl.ds(start, size)
        return remote(halves[i].at[1 - y, rows], items[i].at[y, rows], send.at[at], recv.at[at], across_y)

    def keep(i):
        return pltpu.make_async_copy(halves[i].at[y], items[i].at[y], local.at[i])

    def ship(i):
        return pltpu.make_async_copy(items[i], outs[i], local.at[i])

    def begin(at):
        crossing(at).start()
        if pieces[at][1] == 0:
            keep(pieces[at][0]).start()

    def arrive():
        for at in range(len(pieces)):
            crossing(at).wait()
        for i in range(len(halves)):
            keep(i).wait()
            ship(i).start()

    def finish():
        for i in range(len(halves)):
            ship(i).wait()

    return [functools.partial(begin, at) for at in range(len(pieces))], [arrive, finish]


def peers_along(axis):
    z, x, core, y = position()
    *along, across_x, across_y, across_core = partners()
    if axis == "z":
        return [(other, (z + k + 1) % grid_z) for k, other in enumerate(along)]
    return [{"x": (across_x, 1 - x), "y": (across_y, 1 - y), "c": (across_core, 1 - core)}[axis]]


class LateSwap:
    def __init__(self, values, item, sems, pieces):
        local, send, recv = sems
        y = position()[3]
        half = values.shape[0] // 2
        size = half // pieces

        def crossing(at):
            source = values.at[pl.ds(pl.multiple_of((1 - y) * half + at * size, size), size)]
            return remote(source, item.at[y, pl.ds(at * size, size)], send.at[at], recv.at[at], partners()[4])

        def keep():
            return pltpu.make_async_copy(values.at[pl.ds(pl.multiple_of(y * half, half), half)], item.at[y], local.at[0])

        self.crossing, self.keep, self.pieces = crossing, keep, pieces

    def begin(self, at):
        if at == 0:
            self.keep().start()
        self.crossing(at).start()

    def finish(self):
        self.keep().wait()
        for at in range(self.pieces):
            self.crossing(at).wait()


def window(where):
    row, rows, column, columns = where
    return pl.ds(row, rows), pl.ds(column, columns)


def gather_steps(groups, shards, outs, fulls, sems):
    local, send, recv = sems
    own_place = dict(zip("zxcy", position()))
    chunks = [chunk for group in groups for chunk in group]
    numbers = []
    for group in groups:
        start = numbers[-1][-1] + 1 if numbers else 0
        numbers.append(list(range(start, start + len(group))))
    first_sem = dict(zip("zxyc", (0, 3, 4, 5)))

    def ref(i, hop):
        weight, where, order = chunks[i]
        at = [slice(None) if axis in order[:hop] else own_place[axis] for axis in "zxcy"]
        return fulls[weight].at[(*at, *window(where))]

    def source(i):
        weight, where, _ = chunks[i]
        return shards[weight].at[window(where)]

    def keep(i):
        return pltpu.make_async_copy(source(i), ref(i, 0), local.at[i])

    def ship(i):
        return pltpu.make_async_copy(ref(i, 4), outs[chunks[i][0]].at[(*[slice(None)] * 4, *window(chunks[i][1]))], local.at[i])

    def hops(i, hop):
        axis = chunks[i][2][hop]
        where = first_sem[axis]
        return [
            remote(
                source(i) if hop == 0 else ref(i, hop), ref(i, hop), send.at[i, where + k], recv.at[i, where + k], other
            )
            for k, (other, _) in enumerate(peers_along(axis))
        ]

    def begin():
        for i in range(len(chunks)):
            for copy in (keep(i), *hops(i, 0)):
                copy.start()

    def advance(step):
        for hop in range(4):
            if 0 <= step - hop * lag < len(groups):
                for i in numbers[step - hop * lag]:
                    if hop == 0:
                        keep(i).wait()
                    for copy in hops(i, hop):
                        copy.wait_recv()
                    if hop < 3:
                        for copy in hops(i, hop + 1):
                            copy.start()
                    else:
                        ship(i).start()

    def finish():
        for i in range(len(chunks)):
            for hop in range(4):
                for copy in hops(i, hop):
                    copy.wait_send()
            ship(i).wait()

    return [begin, *(functools.partial(advance, step) for step in range(len(groups) + 3 * lag))], [finish]


def scatter_steps(groups, grads, outs, buffers, sems):
    mine, chip, *came = buffers
    local, send, recv = sems
    place = dict(zip("zxcy", position()))
    sizes = dict(zip("zxy", (grid_z, grid_x, grid_y)))
    first_sem = dict(zip("cxyz", (0, 1, 2, 3)))
    chunks = [chunk for group in groups for chunk in group]
    numbers = []
    for group in groups:
        start = numbers[-1][-1] + 1 if numbers else 0
        numbers.append(list(range(start, start + len(group))))

    def chip_hop(i):
        weight, where, _ = chunks[i]
        source = grads[weight].at[(slice(None), slice(None), 1 - place["c"], slice(None), *window(where))]
        return remote(source, chip[i], send.at[i, 0], recv.at[i, 0], partners()[-1])

    def keep(i):
        weight, where, _ = chunks[i]
        source = grads[weight].at[(slice(None), slice(None), place["c"], slice(None), *window(where))]
        return pltpu.make_async_copy(source, mine[i], local.at[i])

    def left(i, hop):
        return [axis for axis in "zxy" if axis not in chunks[i][2][:hop]]

    def held(i, hop):
        return chip[i] if hop == 0 else came[hop - 1][i].at[0]

    def hops(i, hop):
        axis = chunks[i][2][hop]
        copies = []
        for k, (other, there) in enumerate(peers_along(axis)):
            at = tuple(there if one == axis else slice(None) for one in left(i, hop))
            where = first_sem[axis] + k
            copies.append(
                remote(held(i, hop).at[at], came[hop][i].at[k], send.at[i, where], recv.at[i, where], other)
            )
        return copies

    def begin():
        for i in range(len(chunks)):
            chip_hop(i).start()
        for i in range(min(kept_slots, len(chunks))):
            keep(i).start()

    def after_chip(i):
        keep(i).wait()
        chip_hop(i).wait_recv()

        def add(*at):
            chip[i][at] += mine[i][at]

        each((grid_z, grid_x, grid_y), add)
        for copy in hops(i, 0):
            copy.start()
        if i + kept_slots < len(chunks):
            keep(i + kept_slots).start()

    def after(i, hop):
        weight, window_at, order = chunks[i]
        for copy in hops(i, hop):
            copy.wait_recv()
        axis = order[hop]
        before, rest = left(i, hop), left(i, hop + 1)
        count = sizes[axis] - 1

        def value(*at):
            where = dict(zip(rest, at))
            where[axis] = place[axis]
            own = held(i, hop)[tuple(where[one] for one in before)]
            if count == 1 and rest:
                return own + came[hop][i][(0, *at)]
            total = own.astype(jnp.float32)
            for k in range(count):
                total = total + came[hop][i][(k, *at)].astype(jnp.float32)
            return total

        if rest:

            def add(*at):
                came[hop][i][(0, *at)] = value(*at).astype(jnp.bfloat16)

            each([sizes[one] for one in rest], add)
            for copy in hops(i, hop + 1):
                copy.start()
        else:
            outs[weight][window(window_at)] = value()

    def advance(step):
        for stage in range(4):
            if 0 <= step - stage * lag < len(groups):
                for i in numbers[step - stage * lag]:
                    if stage == 0:
                        after_chip(i)
                    else:
                        after(i, stage - 1)

    def finish():
        for i in range(len(chunks)):
            for copy in (chip_hop(i), *(copy for hop in range(3) for copy in hops(i, hop))):
                copy.wait_send()

    return [begin, *(functools.partial(advance, step) for step in range(len(groups) + 3 * lag))], [finish]


def reduce_steps(fill, total, came, send, recv, finish):
    *along, across_x, across_y, across_core = partners()
    singles = (across_core, across_x, across_y)

    def single(k):
        return remote(total.at[k], came.at[k], send.at[k], recv.at[k], singles[k])

    def line(k):
        return remote(total.at[3], came.at[3 + k], send.at[3 + k], recv.at[3 + k], along[k])

    def begin():
        fill()
        single(0).start()

    def add(k):
        single(k).wait()
        total[k + 1] = total[k] + came[k]
        if k < 2:
            single(k + 1).start()
        else:
            for j in range(grid_z - 1):
                line(j).start()

    def end():
        value = total[3]
        for j in range(grid_z - 1):
            line(j).wait()
            value = value + came[3 + j]
        total[4] = value
        finish()

    return [begin, *(functools.partial(add, k) for k in range(3)), end]


class Moves:
    def __init__(self, gathers=(), gather_groups=(), scatters=(), scatter_groups=(), swaps=()):
        blocks = grid_z * grid_x * grid_core * grid_y
        self.gather_groups, self.scatter_groups = gather_groups, scatter_groups
        gather_chunks = [chunk for group in gather_groups for chunk in group]
        scatter_chunks = [chunk for group in scatter_groups for chunk in group]
        self.scatter_count = len(scatter_chunks)
        self.counts = (len(gathers), len(scatters), len(swaps))
        views = [grad.reshape(block_grid + (grad.shape[0] // blocks, grad.shape[1])) for grad in scatters]
        self.operands = [*gathers, *views, *swaps]
        anywhere = pl.BlockSpec(memory_space=pl.ANY)
        self.in_specs = [anywhere] * len(self.operands)
        rows = [view.shape[-2:] for view in views]
        self.out_specs = (
            [anywhere] * len(gathers)
            + [pl.BlockSpec(shape, lambda *at: (0, 0)) for shape in rows]
            + [anywhere] * len(swaps)
        )
        self.out_shape = (
            [jax.ShapeDtypeStruct(block_grid + shard.shape, shard.dtype) for shard in gathers]
            + [jax.ShapeDtypeStruct(shape, jnp.float32) for shape in rows]
            + [jax.ShapeDtypeStruct(values.shape, values.dtype) for values in swaps]
        )
        sizes = [where[1::2] for _, where, _ in scatter_chunks]
        self.slots = {}
        self.scratch_shapes = []
        for i, size in enumerate(sizes):
            if i < kept_slots or sizes[i - kept_slots] != size:
                self.slots[i] = len(self.scratch_shapes)
                self.scratch_shapes.append(pltpu.VMEM((4, 2, 2) + size, jnp.bfloat16))
            else:
                self.slots[i] = self.slots[i - kept_slots]
        self.kept = len(self.scratch_shapes)
        self.scratch_shapes += [pltpu.VMEM((4, 2, 2) + size, jnp.bfloat16) for size in sizes]
        extents = dict(zip("zxy", (grid_z, grid_x, grid_y)))
        for hop in range(3):
            for (_, _, order), size in zip(scatter_chunks, sizes):
                lead = [extents[order[hop]] - 1] + [extents[one] for one in "zxy" if one not in order[: hop + 1]]
                self.scratch_shapes.append(pltpu.VMEM((*lead, *size), jnp.bfloat16))
        self.scratch_shapes += [pltpu.VMEM(block_grid + shard.shape, shard.dtype) for shard in gathers]
        self.scratch_shapes += [pltpu.VMEM(values.shape, values.dtype) for values in swaps]
        for count, hops in ((len(gather_chunks), 6), (len(scatter_chunks), 6)):
            if count:
                self.scratch_shapes += [
                    pltpu.SemaphoreType.DMA((count,)),
                    pltpu.SemaphoreType.DMA((count, hops)),
                    pltpu.SemaphoreType.DMA((count, hops)),
                ]
        if swaps:
            pieces = sum(len(pieces_of(values.shape[1])) for values in swaps)
            self.scratch_shapes += [pltpu.SemaphoreType.DMA((count,)) for count in (len(swaps), pieces, pieces)]

    def steps(self, ins, outs, scratch):
        gathers, scatters, swaps = self.counts
        scratch = list(scratch)

        def take(count):
            taken = scratch[:count]
            del scratch[:count]
            return taken

        kept = take(self.kept)
        buffers = [[kept[self.slots[i]] for i in range(self.scatter_count)]]
        buffers += [take(self.scatter_count) for _ in range(4)]
        fulls, items = take(gathers), take(swaps)
        lists = []
        if gathers:
            lists.append(gather_steps(self.gather_groups, ins[:gathers], outs[:gathers], fulls, take(3)))
        if scatters:
            span = slice(gathers, gathers + scatters)
            lists.append(scatter_steps(self.scatter_groups, ins[span], outs[span], buffers, take(3)))
        if swaps:
            lists.append(swap_steps(ins[gathers + scatters :], outs[gathers + scatters :], items, take(3)))
        steps = [meet]
        for group in itertools.zip_longest(*(begin for begin, _ in lists)):
            steps.append(functools.partial(call_all, [one for one in group if one is not None]))
        steps[:2] = [functools.partial(call_all, steps[:2])]
        ends = [end[0] for _, end in lists] + [one for _, end in lists for one in end[1:]]
        steps.append(functools.partial(call_all, ends))
        return steps


def call_all(functions):
    for function in functions:
        function()


def carried(body, moves, *, grid, in_specs, out_specs, out_shape, scratch_shapes, ident, name, last=None, tail=0):
    if moves is None:
        run = pl.pallas_call(
            body,
            grid=grid,
            in_specs=in_specs,
            out_specs=out_specs,
            out_shape=out_shape,
            scratch_shapes=scratch_shapes,
            compiler_params=pltpu.CompilerParams(vmem_limit_bytes=48 * 1024 * 1024),
            name=name,
        )
        return lambda *operands: (run(*operands), ())
    counts = [len(in_specs), len(moves.in_specs), len(out_specs), len(moves.out_specs), len(scratch_shapes)]

    def kernel(*refs):
        refs = list(refs)
        parts = []
        for count in counts:
            parts.append(refs[:count])
            del refs[:count]
        ins, move_ins, outs, move_outs, scratch = parts
        steps = moves.steps(move_ins, move_outs, refs)
        size = 1
        for extent in grid:
            size *= extent
        at = pl.program_id(0)
        early = len(steps) - tail
        for i in range(size):
            group = [steps[k] for k in range(early) if k * size // early == i]
            if group:
                pl.when(at == i)(functools.partial(call_all, group))
        if body is not None:
            body(*ins, *outs, *scratch)
        late = [steps[early:]]
        if last is not None:
            late.append(last(*ins, *outs, *scratch))
        order = [one for pairs in itertools.zip_longest(*late) for one in pairs if one is not None]
        if order:
            pl.when(at == size - 1)(functools.partial(call_all, order))

    call = pl.pallas_call(
        kernel,
        grid=grid,
        in_specs=[*in_specs, *moves.in_specs],
        out_specs=[*out_specs, *moves.out_specs],
        out_shape=[*out_shape, *moves.out_shape],
        scratch_shapes=[*scratch_shapes, *moves.scratch_shapes],
        compiler_params=pltpu.CompilerParams(
            collective_id=ident, has_side_effects=True, vmem_limit_bytes=60 * 1024 * 1024
        ),
        name=name,
    )

    def run(*operands):
        results = call(*operands, *moves.operands)
        return results[: len(out_shape)], results[len(out_shape) :]

    return run


def cuts(weights, orders, most=24 * 384):
    groups = []
    for index, (rows, columns) in enumerate(weights):
        if rows % 16 == 0:
            pieces = [(row, 16, 0, columns) for row in range(0, rows, 16)]
        else:
            wide = max(most // rows // pair, 1) * pair
            pieces = [(0, rows, column, min(wide, columns - column)) for column in range(0, columns, wide)]
        for piece in pieces:
            groups.append(((index, piece, orders[len(groups) % len(orders)]),))
    return tuple(groups)


def shard_shapes(grads):
    blocks = grid_z * grid_x * grid_core * grid_y
    return [(grad.shape[0] // blocks, grad.shape[1]) for grad in grads]


def rms_backward(values, gain, grad):
    scale = lax.rsqrt(jnp.mean(values * values, axis=-1, keepdims=True) + epsilon)
    weighted = grad * gain
    inner = jnp.mean(values * weighted, axis=-1, keepdims=True)
    return scale * weighted - values * (scale * scale * scale * inner), jnp.sum(grad * values * scale, axis=0)


def fits(mesh):
    return mesh.shape["dp"] == grid_z * grid_x * grid_core and mesh.shape["seq"] == grid_y


def item_body(
    hidden,
    encoded,
    cotangent,
    w_self_qkv,
    w_self_out,
    w_cross_q,
    w_cross_kv,
    w_cross_out,
    w_ffn_in,
    w_ffn_out,
    norm_gains,
    bucket_bias_matrix,
    dec_lengths,
    ident_tags,
    ident_mask,
    bucket_ids,
):
    width = hidden.shape[2]
    heads = bucket_bias_matrix.shape[1]
    bucket_count = bucket_bias_matrix.shape[0]
    axes = ("dp", "seq")
    place = lax.axis_index("seq")
    both_ids = jnp.broadcast_to(bucket_ids.astype(jnp.bfloat16), (2,) + bucket_ids.shape)
    lanes = (jnp.arange(pair) % (pair // 2) == 0).astype(jnp.float32)
    tags = jnp.where(ident_tags[..., None] == 0, 0.0, masked_score * lanes).astype(jnp.bfloat16)
    group = (w_self_qkv, w_cross_kv, w_self_out, w_cross_q, w_cross_out)
    *weights, own_hidden, ids, tags, own_encoded = bring(
        Moves(
            group,
            cuts([weight.shape for weight in group], ["yzxc"]),
            swaps=[hidden, both_ids, tags, encoded],
        )
    )
    tag_lanes = tags.reshape(-1, pair)
    wqkv, wckv, wso, wcq, wco = (weight.reshape(width, -1) for weight in weights)
    enc_rows = own_encoded.reshape(-1, width)
    states = own_hidden.reshape(-1, width)
    ids = ids.reshape(-1, ids.shape[-1])
    length = jnp.broadcast_to(lax.dynamic_index_in_dim(dec_lengths, place, 0, keepdims=True), (8, pair))
    marks = lax.dynamic_index_in_dim(ident_mask, place, 0, keepdims=False)
    table = jnp.concatenate(
        [
            jnp.transpose(bucket_bias_matrix),
            jnp.full((heads, pair - bucket_count), masked_score, jnp.float32),
        ],
        axis=1,
    ).reshape(heads // 2, 2, pair)
    mark_lanes = jnp.where(marks[:, None] == 1, 0.0, lanes[None, :]).astype(jnp.bfloat16)

    group = (w_ffn_in, w_ffn_out)
    kept, (slse, clse), (win, wout, own_cotangent) = attention_forward(
        length, ids, tag_lanes, mark_lanes, table, norm_gains, states, wqkv, enc_rows, wso, wcq, wckv, wco,
        Moves(group, cuts([weight.shape for weight in group], ["yzxc", "zxyc"]), swaps=[cotangent]),
    )
    win = win.reshape(width, -1)
    wout = wout.reshape(-1, width)
    grad_low = own_cotangent.reshape(-1, width)
    grad_top = grad_low.astype(jnp.float32)
    after_cross, normed_three = kept.x2, kept.n3
    pre = matmul(normed_three, win)
    act = smooth_gelu(pre).astype(jnp.bfloat16)
    block_out = (after_cross + matmul(act, wout)).astype(jnp.bfloat16)

    halves = (2, -1, width)
    grad_wout = contract_rows(act, grad_low).astype(jnp.bfloat16)
    grad_act = contract_cols(grad_low, wout)
    grad_pre = jax.vjp(smooth_gelu, pre)[1](grad_act)[0].astype(jnp.bfloat16)
    grad_win = contract_rows(normed_three, grad_pre).astype(jnp.bfloat16)
    back, gain_three = rms_backward(after_cross, norm_gains[2], contract_cols(grad_pre, win))
    grad_cross = grad_top + back
    cross_low = grad_cross.astype(jnp.bfloat16)
    grad_wco = contract_rows(kept.catt, cross_low).astype(jnp.bfloat16)
    grad_catt = contract_cols(cross_low, wco).astype(jnp.bfloat16)
    grads = [grad_wout, grad_win, grad_wco]
    outs, (sum_wout, sum_win, sum_wco, block_out) = attention_backward(
        kept.cq, kept.ckv, tag_lanes, mark_lanes, grad_catt, kept.cfull, clse,
        kept.qkv, kept.ids_t, table, kept.sfull, slse,
        norm_gains, states, kept.x1, grad_cross, kept.n1, kept.n2, kept.att, enc_rows,
        wcq, wso, wckv, wqkv,
        Moves(
            scatters=grads,
            scatter_groups=cuts(shard_shapes(grads), ["xzy", "xzy", "xzy", "yxz"]),
            swaps=[block_out.reshape(halves)],
        ),
    )
    grad_scores, grad_wqkv, grad_wckv, grad_wcq, grad_wso, grad_enc, grad_inputs, gain_rows = outs
    gains = jnp.concatenate([gain_rows[0], gain_rows[1], gain_three])
    rows = -(-gains.shape[0] // (8 * pair)) * 8
    gains = jnp.pad(gains, (0, rows * pair - gains.shape[0])).reshape(rows, pair)
    grads = [grad_wckv, grad_wcq, grad_wso, grad_wqkv]
    (small,), (sum_wckv, sum_wcq, sum_wso, sum_wqkv) = table_sums(
        gains,
        kept.ids_t,
        grad_scores,
        bucket_count,
        Moves(
            scatters=grads,
            scatter_groups=cuts(shard_shapes(grads), ["xzy", "yxz"]),
        ),
    )
    results = deliver(
        [block_out, grad_inputs, grad_enc, sum_wqkv, sum_wso, sum_wcq, sum_wckv, sum_wco, sum_win, sum_wout]
    )
    gains = small[:rows].reshape(-1)[: 3 * width].reshape(3, width)
    grad_table = small[rows:, :heads]
    return (*results, gains, grad_table)


def solution(mesh):
    placed = (
        P("dp", "seq", None),
        P("dp", "seq", None),
        P("dp", "seq", None),
        P(("dp", "seq"), None),
        P(("dp", "seq"), None),
        P(("dp", "seq"), None),
        P(("dp", "seq"), None),
        P(("dp", "seq"), None),
        P(("dp", "seq"), None),
        P(("dp", "seq"), None),
        P(),
        P(),
        P("dp"),
        P("dp", "seq"),
        P("dp", None),
        P("seq", None),
    )

    def body(*arrays):
        items = arrays[0].shape[0]
        if items == 2 and lax.axis_size("seq") == 2 and fits(mesh):
            return item_body(*arrays)
        return split_body(*arrays)

    return jax.shard_map(
        body,
        mesh=mesh,
        in_specs=placed,
        out_specs=(
            P("dp", "seq", None),
            P("dp", "seq", None),
            P("dp", "seq", None),
            P(("dp", "seq"), None),
            P(("dp", "seq"), None),
            P(("dp", "seq"), None),
            P(("dp", "seq"), None),
            P(("dp", "seq"), None),
            P(("dp", "seq"), None),
            P(("dp", "seq"), None),
            P(),
            P(),
        ),
        check_vma=False,
    )
```

```python
import functools
import itertools
import typing

import jax
import jax.numpy as jnp
from jax import lax
from jax.experimental import pallas as pl
from jax.experimental.pallas import tpu as pltpu
from jax.sharding import PartitionSpec as P

epsilon = 1e-06
score_scale = 0.125
masked_score = -1e30
gelu_coeff = 0.7978845608028654
cubic_coeff = 0.044715


def rms_norm(values, gain):
    return values * lax.rsqrt(jnp.mean(values * values, axis=-1, keepdims=True) + epsilon) * gain


def smooth_gelu(values):
    return (
        0.5
        * values
        * (1.0 + jnp.tanh(gelu_coeff * (values + cubic_coeff * values * values * values)))
    )


def matmul(left, right):
    return jnp.dot(left, right, preferred_element_type=jnp.float32)


def contract_rows(left, right):
    return lax.dot_general(
        left, right, (((0,), (0,)), ((), ())), preferred_element_type=jnp.float32
    )


def contract_cols(left, right):
    return lax.dot_general(
        left, right, (((1,), (1,)), ((), ())), preferred_element_type=jnp.float32
    )


def masked_scores(query, keys, bias, mask):
    scores = (
        jnp.einsum("iqhe,ikhe->ihqk", query, keys, preferred_element_type=jnp.float32) * score_scale
    )
    scores = scores + bias
    return jnp.where(mask[:, None], scores, masked_score)


def attend_forward(query, keys, values, bias, mask):
    scores = masked_scores(query, keys, bias, mask)
    top = jnp.max(scores, axis=-1, keepdims=True)
    expo = jnp.exp(scores - top)
    total = jnp.sum(expo, axis=-1, keepdims=True)
    probs = (expo / total).astype(jnp.bfloat16)
    output = jnp.einsum("ihqk,ikhe->iqhe", probs, values, preferred_element_type=jnp.float32)
    return (output.astype(jnp.bfloat16), top + jnp.log(total))


def attend_backward(query, keys, values, bias, mask, log_total, grad_out):
    probs = jnp.exp(masked_scores(query, keys, bias, mask) - log_total)
    grad_probs = jnp.einsum("iqhe,ikhe->ihqk", grad_out, values, preferred_element_type=jnp.float32)
    grad_values = jnp.einsum(
        "ihqk,iqhe->ikhe", probs.astype(jnp.bfloat16), grad_out, preferred_element_type=jnp.float32
    )
    inner = jnp.sum(grad_probs * probs, axis=-1, keepdims=True)
    grad_scores = (probs * (grad_probs - inner)).astype(jnp.bfloat16)
    grad_query = (
        jnp.einsum("ihqk,ikhe->iqhe", grad_scores, keys, preferred_element_type=jnp.float32)
        * score_scale
    )
    grad_keys = (
        jnp.einsum("ihqk,iqhe->ikhe", grad_scores, query, preferred_element_type=jnp.float32)
        * score_scale
    )
    return (grad_query, grad_keys, grad_values, grad_scores)


def split_body(
    hidden,
    encoded,
    cotangent,
    w_self_qkv,
    w_self_out,
    w_cross_q,
    w_cross_kv,
    w_cross_out,
    w_ffn_in,
    w_ffn_out,
    norm_gains,
    bucket_bias_matrix,
    dec_lengths,
    ident_tags,
    ident_mask,
    bucket_ids,
):
    items, local_dec, width = hidden.shape
    local_enc = encoded.shape[1]
    heads = bucket_bias_matrix.shape[1]
    head_dim = width // heads
    bucket_count = bucket_bias_matrix.shape[0]
    full_dec = local_dec * lax.axis_size("seq")
    full_enc = local_enc * lax.axis_size("seq")
    device_count = lax.axis_size("dp") * lax.axis_size("seq")
    query_pos = lax.axis_index("seq") * local_dec + jnp.arange(local_dec)
    key_pos = jnp.arange(full_dec)
    self_mask = (key_pos[None, None, :] <= query_pos[None, :, None]) & (
        key_pos[None, None, :] < dec_lengths[:, None, None]
    )
    cross_mask = (ident_tags[:, :, None] == 0) | (ident_mask[:, None, :] == 1)
    bucket_indicator = (bucket_ids[None, :, :] == jnp.arange(bucket_count)[:, None, None]).astype(
        jnp.float32
    )
    self_attention_bias = jnp.einsum(
        "ufp,uo->ofp", bucket_indicator, bucket_bias_matrix, precision=lax.Precision.HIGHEST
    )
    inputs = hidden.reshape(-1, width).astype(jnp.float32)
    enc_rows = encoded.reshape(-1, width)

    def forward_pass(weights):
        wqkv, wso, wcq, wckv, wco, win, wout = weights
        normed = rms_norm(inputs, norm_gains[0]).astype(jnp.bfloat16)
        qkv = matmul(normed, wqkv).astype(jnp.bfloat16)
        query = qkv[:, :width].reshape(items, local_dec, heads, head_dim)
        local_kv = qkv[:, width:].reshape(items, local_dec, 2 * width)
        all_kv = lax.all_gather(local_kv, "seq", axis=1, tiled=True)
        keys = all_kv[:, :, :width].reshape(items, full_dec, heads, head_dim)
        values = all_kv[:, :, width:].reshape(items, full_dec, heads, head_dim)
        attended, self_lse = attend_forward(query, keys, values, self_attention_bias, self_mask)
        attended = attended.reshape(-1, width)
        after_self = inputs + matmul(attended, wso)
        normed_two = rms_norm(after_self, norm_gains[1]).astype(jnp.bfloat16)
        local_cq = matmul(normed_two, wcq).astype(jnp.bfloat16)
        local_ckv = matmul(enc_rows, wckv).astype(jnp.bfloat16).reshape(items, local_enc, 2 * width)
        cross_query = local_cq.reshape(items, local_dec, heads, head_dim)
        all_ckv = lax.all_gather(local_ckv, "seq", axis=1, tiled=True)
        cross_keys = all_ckv[:, :, :width].reshape(items, full_enc, heads, head_dim)
        cross_values = all_ckv[:, :, width:].reshape(items, full_enc, heads, head_dim)
        cross_att, cross_lse = attend_forward(
            cross_query, cross_keys, cross_values, 0.0, cross_mask
        )
        cross_att = cross_att.reshape(-1, width)
        after_cross = after_self + matmul(cross_att, wco)
        normed_three = rms_norm(after_cross, norm_gains[2]).astype(jnp.bfloat16)
        pre = matmul(normed_three, win)
        act = smooth_gelu(pre).astype(jnp.bfloat16)
        result = after_cross + matmul(act, wout)
        return dict(
            normed=normed,
            qkv=qkv,
            query=query,
            keys=keys,
            values=values,
            attended=attended,
            self_lse=self_lse,
            after_self=after_self,
            normed_two=normed_two,
            cross_query=cross_query,
            cross_keys=cross_keys,
            cross_values=cross_values,
            cross_att=cross_att,
            cross_lse=cross_lse,
            cross_part_mask=cross_mask,
            after_cross=after_cross,
            normed_three=normed_three,
            pre=pre,
            act=act,
            result=result,
        )

    shards = (w_self_qkv, w_self_out, w_cross_q, w_cross_kv, w_cross_out, w_ffn_in, w_ffn_out)
    first = (
        lax.all_gather(shards[0], ("dp", "seq"), axis=0, tiled=True),
        lax.all_gather(shards[1], ("dp", "seq"), axis=0, tiled=True),
        lax.all_gather(shards[2], ("dp", "seq"), axis=0, tiled=True),
        lax.all_gather(shards[3], ("dp", "seq"), axis=0, tiled=True),
        lax.all_gather(shards[4], ("dp", "seq"), axis=0, tiled=True),
        lax.all_gather(shards[5], ("dp", "seq"), axis=0, tiled=True),
        lax.all_gather(shards[6], ("dp", "seq"), axis=0, tiled=True),
    )
    state = forward_pass(first)
    output = state["result"]
    weights = first
    weights = (
        lax.all_gather(shards[0], ("dp", "seq"), axis=0, tiled=True),
        lax.all_gather(shards[1], ("dp", "seq"), axis=0, tiled=True),
        lax.all_gather(shards[2], ("dp", "seq"), axis=0, tiled=True),
        lax.all_gather(shards[3], ("dp", "seq"), axis=0, tiled=True),
        lax.all_gather(shards[4], ("dp", "seq"), axis=0, tiled=True),
        lax.all_gather(shards[5], ("dp", "seq"), axis=0, tiled=True),
        lax.all_gather(shards[6], ("dp", "seq"), axis=0, tiled=True),
    )
    state = forward_pass(weights)
    wqkv, wso, wcq, wckv, wco, win, wout = weights
    grad_top = cotangent.reshape(-1, width).astype(jnp.float32)
    grad_low = grad_top.astype(jnp.bfloat16)
    grad_wout = contract_rows(state["act"], grad_low)
    grad_act = contract_cols(grad_low, wout)
    grad_pre = jax.vjp(smooth_gelu, state["pre"])[1](grad_act)[0].astype(jnp.bfloat16)
    grad_win = contract_rows(state["normed_three"], grad_pre)
    normalized_gradient = contract_cols(grad_pre, win)
    norm_back, gain_three = jax.vjp(rms_norm, state["after_cross"], norm_gains[2])[1](
        normalized_gradient
    )
    cross_attention_gradient = grad_top + norm_back
    cross_low = cross_attention_gradient.astype(jnp.bfloat16)
    grad_wco = contract_rows(state["cross_att"], cross_low)
    grad_catt_local = contract_cols(cross_low, wco).astype(jnp.bfloat16)
    grad_catt = grad_catt_local.reshape(items, local_dec, heads, head_dim)
    grad_cq, grad_ck, grad_cv, unused_scores = attend_backward(
        state["cross_query"],
        state["cross_keys"],
        state["cross_values"],
        0.0,
        cross_mask,
        state["cross_lse"],
        grad_catt,
    )
    grad_ckv_terms = jnp.concatenate(
        [grad_ck.reshape(items, full_enc, width), grad_cv.reshape(items, full_enc, width)], axis=-1
    )
    grad_ckv = lax.psum_scatter(
        grad_ckv_terms.astype(jnp.bfloat16), "seq", scatter_dimension=1, tiled=True
    ).reshape(-1, 2 * width)
    grad_cq_low = grad_cq.reshape(-1, width).astype(jnp.bfloat16)
    grad_wckv = contract_rows(enc_rows, grad_ckv)
    grad_enc = contract_cols(grad_ckv, wckv).astype(jnp.bfloat16).reshape(encoded.shape)
    grad_wcq = contract_rows(state["normed_two"], grad_cq_low)
    second_normalized_gradient = contract_cols(grad_cq_low, wcq)
    norm_back_two, gain_two = jax.vjp(rms_norm, state["after_self"], norm_gains[1])[1](
        second_normalized_gradient
    )
    grad_self = cross_attention_gradient + norm_back_two
    self_low = grad_self.astype(jnp.bfloat16)
    grad_wso = contract_rows(state["attended"], self_low)
    grad_att = (
        contract_cols(self_low, wso).astype(jnp.bfloat16).reshape(items, local_dec, heads, head_dim)
    )
    grad_q, grad_k, grad_v, grad_scores = attend_backward(
        state["query"],
        state["keys"],
        state["values"],
        self_attention_bias,
        self_mask,
        state["self_lse"],
        grad_att,
    )
    score_totals = jnp.sum(grad_scores.astype(jnp.float32), axis=0)
    bias_gradient = jnp.einsum(
        "xru,pru->xp", bucket_indicator, score_totals, precision=lax.Precision.HIGHEST
    )
    grad_kv_terms = jnp.concatenate(
        [grad_k.reshape(items, full_dec, width), grad_v.reshape(items, full_dec, width)], axis=-1
    )
    grad_kv = lax.psum_scatter(
        grad_kv_terms.astype(jnp.bfloat16), "seq", scatter_dimension=1, tiled=True
    ).reshape(-1, 2 * width)
    grad_qkv = jnp.concatenate([grad_q.reshape(-1, width).astype(jnp.bfloat16), grad_kv], axis=-1)
    grad_wqkv = contract_rows(state["normed"], grad_qkv)
    grad_normed_one = contract_cols(grad_qkv, wqkv)
    norm_back_one, gain_one = jax.vjp(rms_norm, inputs, norm_gains[0])[1](grad_normed_one)
    grad_inputs = (grad_self + norm_back_one).astype(jnp.bfloat16).reshape(hidden.shape)
    full_terms = (grad_wqkv, grad_wso, grad_wcq, grad_wckv, grad_wco, grad_win, grad_wout)
    tiled = tuple((term.reshape(8 * device_count, -1) for term in full_terms))
    summed = (
        lax.psum_scatter(tiled[0], ("dp", "seq"), scatter_dimension=0, tiled=True),
        lax.psum_scatter(tiled[1], ("dp", "seq"), scatter_dimension=0, tiled=True),
        lax.psum_scatter(tiled[2], ("dp", "seq"), scatter_dimension=0, tiled=True),
        lax.psum_scatter(tiled[3], ("dp", "seq"), scatter_dimension=0, tiled=True),
        lax.psum_scatter(tiled[4], ("dp", "seq"), scatter_dimension=0, tiled=True),
        lax.psum_scatter(tiled[5], ("dp", "seq"), scatter_dimension=0, tiled=True),
        lax.psum_scatter(tiled[6], ("dp", "seq"), scatter_dimension=0, tiled=True),
    )
    summed = tuple((piece.reshape(-1, term.shape[1]) for piece, term in zip(summed, full_terms)))
    gain_grads, table_grads = lax.psum(
        (jnp.stack([gain_one, gain_two, gain_three]), bias_gradient), ("dp", "seq")
    )
    block_out = output.astype(jnp.bfloat16).reshape(hidden.shape)
    return (
        block_out,
        grad_inputs,
        grad_enc,
        summed[0],
        summed[1],
        summed[2],
        summed[3],
        summed[4],
        summed[5],
        summed[6],
        gain_grads,
        table_grads,
    )


pair = 128


def nt(left, right):
    return lax.dot_general(left, right, (((1,), (1,)), ((), ())), preferred_element_type=jnp.float32)


masked_bucket = pair - 1


def half_masks():
    lane = lax.broadcasted_iota(jnp.int32, (1, pair), 1)
    low = (lane < pair // 2).astype(jnp.float32).astype(jnp.bfloat16)
    high = (lane >= pair // 2).astype(jnp.float32).astype(jnp.bfloat16)
    return (low, high)


def look_up(row, ids):
    spread = jnp.broadcast_to(row, (ids.shape[0], pair))
    pieces = [
        jnp.take_along_axis(spread, ids[:, at : at + pair], axis=1, mode="promise_in_bounds")
        for at in range(0, ids.shape[1], pair)
    ]
    return jnp.concatenate(pieces, axis=1)


def store_lse(lse_ref, columns):
    lane = lax.broadcasted_iota(jnp.int32, (columns[0].shape[0], pair), 1)
    both = jnp.where(lane == 0, columns[0], columns[1])
    lse_ref[...] = jnp.transpose(both)[: lse_ref.shape[0]]


def attend_rows(scores, values):
    top = jnp.max(scores, axis=1, keepdims=True)
    expo = jnp.exp(scores - top)
    total = jnp.sum(expo, axis=1, keepdims=True)
    output = matmul(expo.astype(jnp.bfloat16), values)
    return output / total, top + jnp.log(total)


def self_forward_kernel(q_ref, k_ref, v_ref, ids_ref, table_ref, att_ref, full_ref, lse_ref, *, block):
    rows = q_ref.shape[0]
    low, high = half_masks()
    lane = lax.broadcasted_iota(jnp.int32, (block, pair), 1)
    columns = ([], [])
    for start in range(0, rows, block):
        span = start + block
        here = slice(start, span)
        query = q_ref[here, :] * jnp.bfloat16(score_scale)
        outs = []
        for side, mask in enumerate((low, high)):
            scores = nt(query * mask, k_ref[:span, :])
            scores = scores + look_up(table_ref[0, side : side + 1, :], ids_ref[here, :span])
            output, lse = attend_rows(scores, v_ref[:span, :])
            outs.append(output)
            columns[side].append(lse)
        both = jnp.where(lane < pair // 2, outs[0], outs[1])
        full_ref[here, :] = both
        att_ref[here, :] = both.astype(jnp.bfloat16)
    store_lse(lse_ref, [jnp.concatenate(column, axis=0) for column in columns])


def cross_forward_kernel(q_ref, k_ref, v_ref, tag_ref, mark_ref, att_ref, full_ref, lse_ref, *, block):
    rows = q_ref.shape[0]
    low, high = half_masks()
    lane = lax.broadcasted_iota(jnp.int32, (block, pair), 1)
    keys = [k_ref[...] * mask + mark_ref[...] * other for mask, other in ((low, high), (high, low))]
    columns = ([], [])
    for start in range(0, rows, block):
        here = slice(start, start + block)
        query = q_ref[here, :] * jnp.bfloat16(score_scale)
        outs = []
        for side, (mask, other) in enumerate(((low, high), (high, low))):
            scores = nt(query * mask + tag_ref[here, :] * other, keys[side])
            output, lse = attend_rows(scores, v_ref[...])
            outs.append(output)
            columns[side].append(lse)
        both = jnp.where(lane < pair // 2, outs[0], outs[1])
        full_ref[here, :] = both
        att_ref[here, :] = both.astype(jnp.bfloat16)
    store_lse(lse_ref, [jnp.concatenate(column, axis=0) for column in columns])


def inner_rows(grad_ref, full_ref):
    product = jnp.transpose(grad_ref[...].astype(jnp.float32) * full_ref[...])
    half = pair // 2
    return [jnp.sum(product[at : at + half], axis=0, keepdims=True) for at in (0, half)]


def backward_chunk(key, key_t, value, query, query_ext, grad, lse, inner, bias):
    scores = nt(key, query_ext)
    if bias is not None:
        scores = scores + bias
    probs = jnp.exp(scores - lse)
    grad_probs = nt(value, grad)
    grad_scores = (probs * (grad_probs - inner)).astype(jnp.bfloat16)
    grad_value = matmul(probs.astype(jnp.bfloat16), grad)
    grad_key = matmul(grad_scores, query)
    grad_query_t = matmul(key_t, grad_scores)
    return grad_scores, grad_value, grad_key, grad_query_t


def rms_rows(values, gain):
    scale = lax.rsqrt(jnp.mean(values * values, axis=1, keepdims=True) + epsilon)
    return (values * scale * gain).astype(jnp.bfloat16)


class Given(typing.NamedTuple):
    length: typing.Any
    ids: typing.Any
    tag: typing.Any
    mark: typing.Any
    table: typing.Any
    gains: typing.Any
    x: typing.Any
    wqkv: typing.Any


class Fetched(typing.NamedTuple):
    enc: typing.Any
    wso: typing.Any
    wcq: typing.Any
    wckv: typing.Any
    wco: typing.Any


class Kept(typing.NamedTuple):
    n1: typing.Any
    ids_t: typing.Any
    qkv: typing.Any
    att: typing.Any
    sfull: typing.Any
    x1: typing.Any
    n2: typing.Any
    cq: typing.Any
    ckv: typing.Any
    catt: typing.Any
    cfull: typing.Any
    x2: typing.Any
    n3: typing.Any


def attention_forward_kernel(*refs, pairs, block):
    refs = list(refs)

    def take(kind):
        taken = kind(*refs[: len(kind._fields)])
        del refs[: len(kind._fields)]
        return taken

    given, distant, kept = take(Given), take(Fetched), take(Kept)
    slse_ref, clse_ref = refs[:2]
    del refs[:2]
    here, near = take(Kept), take(Fetched)
    masked, fetch_sem, keep_sem = refs
    made, wanted = Kept(*range(len(here))), Fetched(*range(len(near)))
    at = pl.program_id(0)
    rows, width = here.att.shape

    def lanes(index):
        return pl.ds(pl.multiple_of(index * pair, pair), pair)

    def columns(panel):
        return slice(panel * width, (panel + 1) * width)

    def fetch(i):
        return pltpu.make_async_copy(distant[i], near[i], fetch_sem.at[i])

    def ship(i):
        return pltpu.make_async_copy(here[i], kept[i], keep_sem.at[i])

    @pl.when(at == 0)
    def _():
        for i in wanted:
            fetch(i).start()
        gain = given.gains[0:1, :]
        length = jnp.where(lax.axis_index("seq") == 0, given.length[0:1, :], given.length[1:2, :])
        for start in range(0, rows, block):
            rest = slice(start, start + block)
            here.n1[rest, :] = rms_rows(given.x[rest, :].astype(jnp.float32), gain)
            for wide in range(0, rows, block):
                query = lax.broadcasted_iota(jnp.int32, (block, block), 0) + start
                key = lax.broadcasted_iota(jnp.int32, (block, block), 1) + wide
                keep = (key <= query) & (key < length)
                ids = given.ids[rest, wide : wide + block].astype(jnp.float32)
                ids = jnp.where(keep, ids, float(masked_bucket))
                masked[rest, wide : wide + block] = ids.astype(jnp.int32)
                here.ids_t[wide : wide + block, rest] = jnp.transpose(ids).astype(jnp.int32)
        ship(made.n1).start()
        ship(made.ids_t).start()

    @pl.when(at == 1)
    def _():
        for panel in range(3):
            product_rows(here.n1, given.wqkv.at[:, columns(panel)], here.qkv.at[:, columns(panel)], 4 * block)
        ship(made.qkv).start()

    @pl.when((at > 1) & (at <= pairs + 1))
    def _():
        index = at - 2
        self_forward_kernel(
            here.qkv.at[:, lanes(index)],
            here.qkv.at[:, lanes(pairs + index)],
            here.qkv.at[:, lanes(2 * pairs + index)],
            masked,
            given.table.at[pl.ds(index, 1)],
            here.att.at[:, lanes(index)],
            here.sfull.at[:, lanes(index)],
            slse_ref,
            block=block,
        )

    @pl.when(at == pairs + 2)
    def _():
        fetch(wanted.wso).wait()
        fetch(wanted.wcq).wait()
        for start in range(0, rows, 2 * block):
            rest = slice(start, start + 2 * block)
            total = given.x[rest, :].astype(jnp.float32) + matmul(here.att[rest, :], near.wso[...])
            here.x1[rest, :] = total
            here.n2[rest, :] = rms_rows(total, given.gains[1:2, :])
        product_rows(here.n2, near.wcq, here.cq, 4 * block)
        for i in (made.att, made.sfull, made.x1, made.n2, made.cq):
            ship(i).start()

    @pl.when(at == pairs + 3)
    def _():
        fetch(wanted.enc).wait()
        fetch(wanted.wckv).wait()
        for panel in range(2):
            product_rows(near.enc, near.wckv.at[:, columns(panel)], here.ckv.at[:, columns(panel)], 4 * block)
        ship(made.ckv).start()

    @pl.when((at > pairs + 3) & (at <= 2 * pairs + 3))
    def _():
        index = at - pairs - 4
        cross_forward_kernel(
            here.cq.at[:, lanes(index)],
            here.ckv.at[:, lanes(index)],
            here.ckv.at[:, lanes(pairs + index)],
            given.tag,
            given.mark,
            here.catt.at[:, lanes(index)],
            here.cfull.at[:, lanes(index)],
            clse_ref,
            block=block,
        )

    @pl.when(at == 2 * pairs + 4)
    def _():
        ship(made.catt).start()
        ship(made.cfull).start()
        fetch(wanted.wco).wait()
        for start in range(0, rows, 2 * block):
            rest = slice(start, start + 2 * block)
            total = here.x1[rest, :] + matmul(here.catt[rest, :], near.wco[...])
            here.x2[rest, :] = total
            here.n3[rest, :] = rms_rows(total, given.gains[2:3, :])
        ship(made.x2).start()
        ship(made.n3).start()
        for i in made:
            ship(i).wait()


def cross_backward_pair(q_ref, k_ref, v_ref, tag_ref, mark_ref, grad_ref, full_ref, lse_ref, query_t, *, block, put):
    low, high = half_masks()
    inner = inner_rows(grad_ref, full_ref)
    query = q_ref[...] * jnp.bfloat16(score_scale)
    queries = [query * low, query * high]
    exts = [queries[0] + tag_ref[...] * high, queries[1] + tag_ref[...] * low]
    grads = [grad_ref[...] * low, grad_ref[...] * high]
    for start in range(0, k_ref.shape[0], block):
        here = slice(start, start + block)
        key = k_ref[here, :]
        parts = [None, None, None]
        for side, (mask, other) in enumerate(((low, high), (high, low))):
            own = key * mask
            _, *news = backward_chunk(
                own + mark_ref[here, :] * other,
                jnp.transpose(own),
                v_ref[here, :],
                queries[side],
                exts[side],
                grads[side],
                lse_ref[side : side + 1, :],
                inner[side],
                None,
            )
            parts = [new if part is None else part + new for part, new in zip(parts, news)]
        put(2, here, parts[0].astype(jnp.bfloat16))
        put(1, here, parts[1].astype(jnp.bfloat16))
        query_t[...] = parts[2] if start == 0 else query_t[...] + parts[2]
    put(0, slice(None), (jnp.transpose(query_t[...]) * score_scale).astype(jnp.bfloat16))


def self_backward_pair(q_ref, k_ref, v_ref, ids_ref, table_ref, grad_ref, full_ref, lse_ref, ds_ref, query_t, *, block, put):
    low, high = half_masks()
    inner = inner_rows(grad_ref, full_ref)
    query = q_ref[...] * jnp.bfloat16(score_scale)
    for start in range(0, k_ref.shape[0], block):
        here = slice(start, start + block)
        key = k_ref[here, :]
        parts = [None, None, None]
        for side, mask in enumerate((low, high)):
            own = query[start:, :] * mask
            scores, *news = backward_chunk(
                key,
                jnp.transpose(key * mask),
                v_ref[here, :],
                own,
                own,
                grad_ref[start:, :] * mask,
                lse_ref[side : side + 1, start:],
                inner[side][:, start:],
                look_up(table_ref[0, side : side + 1, :], ids_ref[here, start:]),
            )
            ds_ref[side, here, start:] = scores
            parts = [new if part is None else part + new for part, new in zip(parts, news)]
        put(2, here, parts[0].astype(jnp.bfloat16))
        put(1, here, parts[1].astype(jnp.bfloat16))
        if start == 0:
            query_t[...] = parts[2]
        else:
            query_t[:, start:] += parts[2]
    put(0, slice(None), (jnp.transpose(query_t[...]) * score_scale).astype(jnp.bfloat16))


def rms_back_rows(values, gain, grad):
    scale = lax.rsqrt(jnp.mean(values * values, axis=1, keepdims=True) + epsilon)
    weighted = grad * gain
    inner = jnp.mean(values * weighted, axis=1, keepdims=True)
    back = scale * weighted - values * (scale * scale * scale * inner)
    return back, jnp.sum(grad * values * scale, axis=0, keepdims=True)


def turn(source, target):
    rows, columns = source.shape
    for start in range(0, columns, pair):
        target[start : start + pair, :rows] = jnp.transpose(source[:, start : start + pair])


def product_rows(left, right, target, most, dims=(((1,), (0,)), ((), ()))):
    rows = target.shape[0]
    block = max(size for size in range(1, most + 1) if rows % size == 0)
    for start in range(0, rows, block):
        here = slice(start, start + block)
        product = lax.dot_general(left[here, :], right[...], dims, preferred_element_type=jnp.float32)
        target[here, :] = product.astype(jnp.bfloat16)


nt_dims = (((1,), (1,)), ((), ()))


def attention_backward_kernel(
    cq_ref,
    ck_ref,
    cv_ref,
    tag_ref,
    mark_ref,
    gcatt_ref,
    cfull_ref,
    clse_ref,
    q_ref,
    k_ref,
    v_ref,
    ids_ref,
    table_ref,
    sfull_ref,
    slse_ref,
    gains_ref,
    x_ref,
    x1_ref,
    gx2_ref,
    n1_ref,
    n2_ref,
    att_ref,
    enc_ref,
    wcq_ref,
    wso_ref,
    wckv_ref,
    wqkv_ref,
    ds_ref,
    gwqkv_ref,
    gwckv_ref,
    gwcq_ref,
    gwso_ref,
    enc_items,
    x_items,
    ggain_ref,
    gcq,
    gckv,
    gqkv,
    gx1,
    low_x1,
    gatt,
    total,
    tall,
    query_t,
    genc,
    gx,
    *swap_sems,
    pairs,
    block,
):
    enc_sems, x_sems = swap_sems[:3], swap_sems[3:]
    at = pl.program_id(0)
    rows, width = gcq.shape
    keys = gckv.shape[0]

    def lanes(first, index):
        return pl.ds(pl.multiple_of(first + index * pair, pair), pair)

    @pl.when(at < pairs)
    def _():
        def put(kind, where, values):
            if kind == 0:
                gcq[where, lanes(0, at)] = values
            else:
                gckv[where, lanes((kind - 1) * width, at)] = values

        cross_backward_pair(
            cq_ref, ck_ref, cv_ref, tag_ref, mark_ref, gcatt_ref, cfull_ref, clse_ref, query_t, block=2 * block, put=put
        )

    @pl.when(at == pairs)
    def _():
        gain = gains_ref[1:2, :]
        sums = None
        for start in range(0, rows, 2 * block):
            here = slice(start, start + 2 * block)
            back, part = rms_back_rows(x1_ref[here, :], gain, nt(gcq[here, :], wcq_ref[...]))
            gx1[here, :] = gx2_ref[here, :] + back
            low_x1[here, :] = gx1[here, :].astype(jnp.bfloat16)
            sums = part if sums is None else sums + part
        ggain_ref[1:2, :] = sums
        product_rows(low_x1, wso_ref, gatt, 4 * block, nt_dims)

    enc_pieces, x_pieces = enc_sems[1].shape[0], x_sems[1].shape[0]
    enc_swap = LateSwap(genc, enc_items, enc_sems, enc_pieces)
    x_swap = LateSwap(gx, x_items, x_sems, x_pieces)

    @pl.when(at == pairs + 1)
    def _():
        product_rows(gckv, wckv_ref, genc, 4 * block, nt_dims)

    for piece in range(enc_pieces):
        pl.when(at == min(pairs + 2 + piece, 2 * pairs + 5))(functools.partial(enc_swap.begin, piece))

    @pl.when((at > pairs + 1) & (at <= 2 * pairs + 1))
    def _():
        index = at - pairs - 2

        def put(kind, where, values):
            gqkv[where, lanes(kind * width, index)] = values

        self_backward_pair(
            q_ref,
            k_ref,
            v_ref,
            ids_ref,
            table_ref,
            gatt.at[:, lanes(0, index)],
            sfull_ref,
            slse_ref,
            ds_ref,
            query_t,
            block=block,
            put=put,
        )

    @pl.when(at == 2 * pairs + 2)
    def _():
        turn(n1_ref, tall)

    for panel in range(3):

        @pl.when(at == 2 * pairs + 2 + panel)
        def _(panel=panel):
            columns = slice(panel * width, (panel + 1) * width)
            product_rows(tall.at[:, :rows], gqkv.at[:, columns], gwqkv_ref, 4 * block)
            for start in range(0, rows, 2 * block):
                here = slice(start, start + 2 * block)
                part = nt(gqkv[here, columns], wqkv_ref[...])
                total[here, :] = part if panel == 0 else total[here, :] + part

    @pl.when(at == 2 * pairs + 4)
    def _():
        gain = gains_ref[0:1, :]
        sums = None
        for start in range(0, rows, block):
            here = slice(start, start + block)
            back, part = rms_back_rows(x_ref[here, :].astype(jnp.float32), gain, total[here, :])
            gx[here, :] = (gx1[here, :] + back).astype(jnp.bfloat16)
            sums = part if sums is None else sums + part
        ggain_ref[0:1, :] = sums
        for piece in range(x_pieces):
            x_swap.begin(piece)

    @pl.when(at == 2 * pairs + 5)
    def _():
        turn(enc_ref, tall)
        for panel in range(2):
            columns = slice(panel * width, (panel + 1) * width)
            product_rows(tall.at[:, :keys], gckv.at[:, columns], gwckv_ref.at[:, columns], 4 * block)

    @pl.when(at == 2 * pairs + 6)
    def _():
        turn(n2_ref, tall)
        product_rows(tall.at[:, :rows], gcq, gwcq_ref, 4 * block)
        turn(att_ref, tall)
        product_rows(tall.at[:, :rows], low_x1, gwso_ref, 4 * block)
        enc_swap.finish()
        x_swap.finish()


def table_kernel(gains_ref, ids_ref, ds_ref, out_ref, sums, spread, table, total, came, send, recv, *, buckets):
    heads, block = ds_ref.shape[0], ds_ref.shape[1]

    @pl.when(pl.program_id(0) == 0)
    def _():
        sums[...] = jnp.zeros_like(sums)

    spread[...] = ds_ref[...].astype(jnp.float32)
    ids = ids_ref[...]

    def step(bucket, carry):
        chosen = ids == bucket
        for head in range(heads):
            picked = jnp.where(chosen, spread[head], 0.0).reshape(block // 8, 8, pair)
            sums[bucket, head] += jnp.sum(picked, axis=0)
        return carry

    lax.fori_loop(0, buckets, step, 0)


def table_finish(gains_ref, ids_ref, ds_ref, out_ref, sums, spread, table, total, came, send, recv):
    heads = ds_ref.shape[0]

    def fill():
        table[...] = jnp.zeros_like(table)
        table[:, :heads] = jnp.sum(jnp.sum(sums[...], axis=3), axis=2)
        total[0] = jnp.concatenate([gains_ref[...], table[...]], axis=0)

    def finish():
        out_ref[...] = total[4]

    return reduce_steps(fill, total, came, send, recv, finish)


def block_of(rows, first=0):
    return pl.BlockSpec((rows, pair), lambda at: (0, first + at))


def whole(shape):
    return pl.BlockSpec(shape, lambda at: (0,) * len(shape))


def attention_forward(length, ids, tag_lanes, mark_lanes, table, gains, states, wqkv, enc, wso, wcq, wckv, wco, moves):
    rows, width = states.shape
    keys = enc.shape[0]
    pairs = width // pair
    low, high = jnp.bfloat16, jnp.float32
    shapes = Kept(
        n1=((rows, width), low),
        ids_t=((rows, rows), jnp.int32),
        qkv=((rows, 3 * width), low),
        att=((rows, width), low),
        sfull=((rows, width), high),
        x1=((rows, width), high),
        n2=((rows, width), low),
        cq=((rows, width), low),
        ckv=((keys, 2 * width), low),
        catt=((rows, width), low),
        cfull=((rows, width), high),
        x2=((rows, width), high),
        n3=((rows, width), low),
    )

    def once(values):
        return pl.BlockSpec(values.shape, lambda at: (0,) * len(values.shape), pipeline_mode=pl.Buffered(1))

    anywhere = pl.BlockSpec(memory_space=pl.ANY)
    given = (length, ids, tag_lanes, mark_lanes, table, gains, states, wqkv)
    distant = (enc, wso, wcq, wckv, wco)
    outs, moved = carried(
        functools.partial(attention_forward_kernel, pairs=pairs, block=128),
        moves,
        grid=(2 * pairs + 5,),
        in_specs=[*(once(values) for values in given), *(anywhere for _ in distant)],
        out_specs=[anywhere] * len(shapes)
        + [
            pl.BlockSpec((8, rows), lambda at: (jnp.clip(at - 2, 0, pairs - 1), 0)),
            pl.BlockSpec((8, rows), lambda at: (jnp.clip(at - pairs - 4, 0, pairs - 1), 0)),
        ],
        out_shape=[jax.ShapeDtypeStruct(*shape) for shape in shapes]
        + [jax.ShapeDtypeStruct((pairs * 8, rows), high)] * 2,
        scratch_shapes=[pltpu.VMEM(*shape) for shape in shapes]
        + [pltpu.VMEM(values.shape, values.dtype) for values in distant]
        + [
            pltpu.VMEM((rows, rows), jnp.int32),
            pltpu.SemaphoreType.DMA((len(distant),)),
            pltpu.SemaphoreType.DMA((len(shapes),)),
        ],
        ident=1,
        name="attention_forward",
        tail=2,
    )(*given, *distant)
    return Kept(*outs[: len(shapes)]), outs[len(shapes) :], moved


def deliver_kernel(*refs):
    count = len(refs) // 3
    sems = refs[-1]
    incoming = [pltpu.make_async_copy(refs[i], refs[2 * count + i], sems.at[i]) for i in range(count)]
    outgoing = [pltpu.make_async_copy(refs[2 * count + i], refs[count + i], sems.at[i]) for i in range(count)]
    for copy in incoming:
        copy.start()
    for one, other in zip(incoming, outgoing):
        one.wait()
        other.start()
    for copy in outgoing:
        copy.wait()


def deliver(results):
    anywhere = pl.BlockSpec(memory_space=pl.ANY)
    return pl.pallas_call(
        deliver_kernel,
        in_specs=[anywhere] * len(results),
        out_specs=[anywhere] * len(results),
        out_shape=[jax.ShapeDtypeStruct(result.shape, result.dtype) for result in results],
        scratch_shapes=[pltpu.VMEM(result.shape, result.dtype) for result in results]
        + [pltpu.SemaphoreType.DMA((len(results),))],
        compiler_params=pltpu.CompilerParams(vmem_limit_bytes=32 * 1024 * 1024),
        name="deliver",
    )(*results)


def attention_backward(
    query, ckv, tag_lanes, mark_lanes, grad_catt, cross_full, cross_lse,
    qkv, ids_t, table, self_full, self_lse,
    gains, states, after_self, grad_cross, normed, normed_two, attended, enc_rows,
    wcq, wso, wckv, wqkv, moves,
):
    rows, width = query.shape
    keys = ckv.shape[0]
    pairs = width // pair
    last = pairs - 1

    def cross_block(count, first=0):
        return pl.BlockSpec((count, pair), lambda at: (0, first + jnp.minimum(at, last)))

    def self_index(at):
        return jnp.clip(at - pairs - 2, 0, last)

    def self_block(count, first=0):
        return pl.BlockSpec((count, pair), lambda at: (0, first + self_index(at)))

    def once(values):
        return pl.BlockSpec(values.shape, lambda at: (0,) * len(values.shape), pipeline_mode=pl.Buffered(1))

    def panel(count):
        return pl.BlockSpec((count, width), lambda at: (0, jnp.clip(at - 2 * pairs - 2, 0, 2)))

    low = jnp.bfloat16
    wholes = [(width, 2 * width), (width, width), (width, width)]
    items = [(2, keys // 2, width), (2, rows // 2, width)]
    return carried(
        functools.partial(attention_backward_kernel, pairs=pairs, block=128),
        moves,
        grid=(2 * pairs + 7,),
        in_specs=[
            cross_block(rows),
            cross_block(keys),
            cross_block(keys, pairs),
            once(tag_lanes),
            once(mark_lanes),
            cross_block(rows),
            cross_block(rows),
            pl.BlockSpec((8, rows), lambda at: (jnp.minimum(at, last), 0)),
            self_block(rows),
            self_block(rows, pairs),
            self_block(rows, 2 * pairs),
            once(ids_t),
            pl.BlockSpec((1, 2, pair), lambda at: (self_index(at), 0, 0)),
            self_block(rows),
            pl.BlockSpec((8, rows), lambda at: (self_index(at), 0)),
            *(
                once(values)
                for values in (gains, states, after_self, grad_cross, normed, normed_two, attended, enc_rows, wcq, wso, wckv)
            ),
            panel(width),
        ],
        out_specs=[
            pl.BlockSpec((2, rows, rows), lambda at: (self_index(at), 0, 0)),
            panel(width),
            *(pl.BlockSpec(shape, lambda at: (0, 0), pipeline_mode=pl.Buffered(1)) for shape in wholes),
            *(pl.BlockSpec(memory_space=pl.ANY) for _ in items),
            pl.BlockSpec((8, width), lambda at: (0, 0)),
        ],
        out_shape=[
            jax.ShapeDtypeStruct((pairs * 2, rows, rows), low),
            jax.ShapeDtypeStruct((width, 3 * width), low),
            *(jax.ShapeDtypeStruct(shape, low) for shape in wholes + items),
            jax.ShapeDtypeStruct((8, width), jnp.float32),
        ],
        scratch_shapes=[
            pltpu.VMEM((rows, width), low),
            pltpu.VMEM((keys, 2 * width), low),
            pltpu.VMEM((rows, 3 * width), low),
            pltpu.VMEM((rows, width), jnp.float32),
            pltpu.VMEM((rows, width), low),
            pltpu.VMEM((rows, width), low),
            pltpu.VMEM((rows, width), jnp.float32),
            pltpu.VMEM((width, keys), low),
            pltpu.VMEM((pair, rows), jnp.float32),
            pltpu.VMEM((keys, width), low),
            pltpu.VMEM((rows, width), low),
            *(pltpu.SemaphoreType.DMA((count,)) for count in (1, 8, 8, 1, 2, 2)),
        ],
        ident=3,
        name="attention_backward",
        tail=0,
    )(
        query, ckv, ckv, tag_lanes, mark_lanes, grad_catt, cross_full, cross_lse,
        qkv, qkv, qkv, ids_t, table, self_full, self_lse,
        gains, states, after_self, grad_cross, normed, normed_two, attended, enc_rows,
        wcq, wso, wckv, wqkv,
    )


def table_sums(gains, ids_t, grad_scores, buckets, moves):
    heads = grad_scores.shape[0]
    side = ids_t.shape[0] // pair
    starts = [sum(side - row for row in range(before)) for before in range(1, side)]

    def place(at):
        row, column = 0, at
        for back, start in enumerate(starts):
            past = jnp.where(at >= start, 1, 0)
            row = row + past
            column = column - past * (side - 1 - back)
        return row, column

    small = (gains.shape[0] + buckets, pair)
    return carried(
        functools.partial(table_kernel, buckets=buckets),
        moves,
        grid=(side * (side + 1) // 2,),
        in_specs=[
            whole(gains.shape),
            pl.BlockSpec((pair, pair), place),
            pl.BlockSpec((heads, pair, pair), lambda at: (0, *place(at))),
        ],
        out_specs=[whole(small)],
        out_shape=[jax.ShapeDtypeStruct(small, jnp.float32)],
        scratch_shapes=[
            pltpu.VMEM((buckets, heads, 8, pair), jnp.float32),
            pltpu.VMEM((heads, pair, pair), jnp.float32),
            pltpu.VMEM((buckets, pair), jnp.float32),
            pltpu.VMEM((5,) + small, jnp.float32),
            pltpu.VMEM((6,) + small, jnp.float32),
            pltpu.SemaphoreType.DMA((6,)),
            pltpu.SemaphoreType.DMA((6,)),
        ],
        ident=5,
        name="table_sums",
        last=table_finish,
        tail=9,
    )(gains, ids_t, grad_scores)


def bring(moves):
    return carried(
        None, moves, grid=(1,), in_specs=[], out_specs=[], out_shape=[], scratch_shapes=[], ident=0, name="bring"
    )()[1]


MESH = pl.DeviceIdType.MESH
grid_z, grid_x, grid_core, grid_y = 4, 2, 2, 2
kept_slots = 3
lag = 2
swap_rows = 128
block_grid = (grid_z, grid_x, grid_core, grid_y)


def position():
    at = lax.axis_index("dp")
    return at // 4, (at // 2) % 2, at % 2, lax.axis_index("seq")


def device_at(z, x, core, y):
    return ((z * grid_x + x) * grid_core + core, y)


def partners():
    z, x, core, y = position()
    along = [device_at((z + step) % grid_z, x, core, y) for step in range(1, grid_z)]
    return along + [device_at(z, 1 - x, core, y), device_at(z, x, core, 1 - y), device_at(z, x, 1 - core, y)]


def meet():
    barrier = pltpu.get_barrier_semaphore()
    others = partners()
    for other in others:
        pl.semaphore_signal(barrier, inc=1, device_id=other, device_id_type=MESH)
    pl.semaphore_wait(barrier, len(others))


def remote(source, target, send, recv, other):
    return pltpu.make_async_remote_copy(
        src_ref=source, dst_ref=target, send_sem=send, recv_sem=recv, device_id=other, device_id_type=MESH
    )


def each(sizes, body):
    total = 1
    for size in sizes:
        total *= size

    def step(at, carry):
        indices = []
        for size in reversed(sizes):
            indices.append(at % size)
            at = at // size
        body(*reversed(indices))
        return carry

    lax.fori_loop(0, total, step, 0)


def pieces_of(rows):
    size = min(rows, swap_rows)
    return [(start, size) for start in range(0, rows, size)]


def swap_steps(halves, outs, items, sems):
    local, send, recv = sems
    y = position()[3]
    across_y = partners()[4]
    pieces = [(i, *piece) for i, half in enumerate(halves) for piece in pieces_of(half.shape[1])]

    def crossing(at):
        i, start, size = pieces[at]
        rows = pl.ds(start, size)
        return remote(halves[i].at[1 - y, rows], items[i].at[y, rows], send.at[at], recv.at[at], across_y)

    def keep(i):
        return pltpu.make_async_copy(halves[i].at[y], items[i].at[y], local.at[i])

    def ship(i):
        return pltpu.make_async_copy(items[i], outs[i], local.at[i])

    def begin(at):
        crossing(at).start()
        if pieces[at][1] == 0:
            keep(pieces[at][0]).start()

    def arrive():
        for at in range(len(pieces)):
            crossing(at).wait()
        for i in range(len(halves)):
            keep(i).wait()
            ship(i).start()

    def finish():
        for i in range(len(halves)):
            ship(i).wait()

    return [functools.partial(begin, at) for at in range(len(pieces))], [arrive, finish]


def peers_along(axis):
    z, x, core, y = position()
    *along, across_x, across_y, across_core = partners()
    if axis == "z":
        return [(other, (z + k + 1) % grid_z) for k, other in enumerate(along)]
    return [{"x": (across_x, 1 - x), "y": (across_y, 1 - y), "c": (across_core, 1 - core)}[axis]]


class LateSwap:
    def __init__(self, values, item, sems, pieces):
        local, send, recv = sems
        y = position()[3]
        half = values.shape[0] // 2
        size = half // pieces

        def crossing(at):
            source = values.at[pl.ds(pl.multiple_of((1 - y) * half + at * size, size), size)]
            return remote(source, item.at[y, pl.ds(at * size, size)], send.at[at], recv.at[at], partners()[4])

        def keep():
            return pltpu.make_async_copy(values.at[pl.ds(pl.multiple_of(y * half, half), half)], item.at[y], local.at[0])

        self.crossing, self.keep, self.pieces = crossing, keep, pieces

    def begin(self, at):
        if at == 0:
            self.keep().start()
        self.crossing(at).start()

    def finish(self):
        self.keep().wait()
        for at in range(self.pieces):
            self.crossing(at).wait()


def window(where):
    row, rows, column, columns = where
    return pl.ds(row, rows), pl.ds(column, columns)


def gather_steps(groups, shards, outs, fulls, sems):
    local, send, recv = sems
    own_place = dict(zip("zxcy", position()))
    chunks = [chunk for group in groups for chunk in group]
    numbers = []
    for group in groups:
        start = numbers[-1][-1] + 1 if numbers else 0
        numbers.append(list(range(start, start + len(group))))
    first_sem = dict(zip("zxyc", (0, 3, 4, 5)))

    def ref(i, hop):
        weight, where, order = chunks[i]
        at = [slice(None) if axis in order[:hop] else own_place[axis] for axis in "zxcy"]
        return fulls[weight].at[(*at, *window(where))]

    def source(i):
        weight, where, _ = chunks[i]
        return shards[weight].at[window(where)]

    def keep(i):
        return pltpu.make_async_copy(source(i), ref(i, 0), local.at[i])

    def ship(i):
        return pltpu.make_async_copy(ref(i, 4), outs[chunks[i][0]].at[(*[slice(None)] * 4, *window(chunks[i][1]))], local.at[i])

    def hops(i, hop):
        axis = chunks[i][2][hop]
        where = first_sem[axis]
        return [
            remote(
                source(i) if hop == 0 else ref(i, hop), ref(i, hop), send.at[i, where + k], recv.at[i, where + k], other
            )
            for k, (other, _) in enumerate(peers_along(axis))
        ]

    def begin():
        for i in range(len(chunks)):
            for copy in (keep(i), *hops(i, 0)):
                copy.start()

    def advance(step):
        for hop in range(4):
            if 0 <= step - hop * lag < len(groups):
                for i in numbers[step - hop * lag]:
                    if hop == 0:
                        keep(i).wait()
                    for copy in hops(i, hop):
                        copy.wait_recv()
                    if hop < 3:
                        for copy in hops(i, hop + 1):
                            copy.start()
                    else:
                        ship(i).start()

    def finish():
        for i in range(len(chunks)):
            for hop in range(4):
                for copy in hops(i, hop):
                    copy.wait_send()
            ship(i).wait()

    return [begin, *(functools.partial(advance, step) for step in range(len(groups) + 3 * lag))], [finish]


def scatter_steps(groups, grads, outs, buffers, sems):
    mine, chip, *came = buffers
    local, send, recv = sems
    place = dict(zip("zxcy", position()))
    sizes = dict(zip("zxy", (grid_z, grid_x, grid_y)))
    first_sem = dict(zip("cxyz", (0, 1, 2, 3)))
    chunks = [chunk for group in groups for chunk in group]
    numbers = []
    for group in groups:
        start = numbers[-1][-1] + 1 if numbers else 0
        numbers.append(list(range(start, start + len(group))))

    def chip_hop(i):
        weight, where, _ = chunks[i]
        source = grads[weight].at[(slice(None), slice(None), 1 - place["c"], slice(None), *window(where))]
        return remote(source, chip[i], send.at[i, 0], recv.at[i, 0], partners()[-1])

    def keep(i):
        weight, where, _ = chunks[i]
        source = grads[weight].at[(slice(None), slice(None), place["c"], slice(None), *window(where))]
        return pltpu.make_async_copy(source, mine[i], local.at[i])

    def left(i, hop):
        return [axis for axis in "zxy" if axis not in chunks[i][2][:hop]]

    def held(i, hop):
        return chip[i] if hop == 0 else came[hop - 1][i].at[0]

    def hops(i, hop):
        axis = chunks[i][2][hop]
        copies = []
        for k, (other, there) in enumerate(peers_along(axis)):
            at = tuple(there if one == axis else slice(None) for one in left(i, hop))
            where = first_sem[axis] + k
            copies.append(
                remote(held(i, hop).at[at], came[hop][i].at[k], send.at[i, where], recv.at[i, where], other)
            )
        return copies

    def begin():
        for i in range(len(chunks)):
            chip_hop(i).start()
        for i in range(min(kept_slots, len(chunks))):
            keep(i).start()

    def after_chip(i):
        keep(i).wait()
        chip_hop(i).wait_recv()

        def add(*at):
            chip[i][at] += mine[i][at]

        each((grid_z, grid_x, grid_y), add)
        for copy in hops(i, 0):
            copy.start()
        if i + kept_slots < len(chunks):
            keep(i + kept_slots).start()

    def after(i, hop):
        weight, window_at, order = chunks[i]
        for copy in hops(i, hop):
            copy.wait_recv()
        axis = order[hop]
        before, rest = left(i, hop), left(i, hop + 1)
        count = sizes[axis] - 1

        def value(*at):
            where = dict(zip(rest, at))
            where[axis] = place[axis]
            own = held(i, hop)[tuple(where[one] for one in before)]
            if count == 1 and rest:
                return own + came[hop][i][(0, *at)]
            total = own.astype(jnp.float32)
            for k in range(count):
                total = total + came[hop][i][(k, *at)].astype(jnp.float32)
            return total

        if rest:

            def add(*at):
                came[hop][i][(0, *at)] = value(*at).astype(jnp.bfloat16)

            each([sizes[one] for one in rest], add)
            for copy in hops(i, hop + 1):
                copy.start()
        else:
            outs[weight][window(window_at)] = value()

    def advance(step):
        for stage in range(4):
            if 0 <= step - stage * lag < len(groups):
                for i in numbers[step - stage * lag]:
                    if stage == 0:
                        after_chip(i)
                    else:
                        after(i, stage - 1)

    def finish():
        for i in range(len(chunks)):
            for copy in (chip_hop(i), *(copy for hop in range(3) for copy in hops(i, hop))):
                copy.wait_send()

    return [begin, *(functools.partial(advance, step) for step in range(len(groups) + 3 * lag))], [finish]


def reduce_steps(fill, total, came, send, recv, finish):
    *along, across_x, across_y, across_core = partners()
    singles = (across_core, across_x, across_y)

    def single(k):
        return remote(total.at[k], came.at[k], send.at[k], recv.at[k], singles[k])

    def line(k):
        return remote(total.at[3], came.at[3 + k], send.at[3 + k], recv.at[3 + k], along[k])

    def begin():
        fill()
        single(0).start()

    def add(k):
        single(k).wait()
        total[k + 1] = total[k] + came[k]
        if k < 2:
            single(k + 1).start()
        else:
            for j in range(grid_z - 1):
                line(j).start()

    def end():
        value = total[3]
        for j in range(grid_z - 1):
            line(j).wait()
            value = value + came[3 + j]
        total[4] = value
        finish()

    return [begin, *(functools.partial(add, k) for k in range(3)), end]


class Moves:
    def __init__(self, gathers=(), gather_groups=(), scatters=(), scatter_groups=(), swaps=()):
        blocks = grid_z * grid_x * grid_core * grid_y
        self.gather_groups, self.scatter_groups = gather_groups, scatter_groups
        gather_chunks = [chunk for group in gather_groups for chunk in group]
        scatter_chunks = [chunk for group in scatter_groups for chunk in group]
        self.scatter_count = len(scatter_chunks)
        self.counts = (len(gathers), len(scatters), len(swaps))
        views = [grad.reshape(block_grid + (grad.shape[0] // blocks, grad.shape[1])) for grad in scatters]
        self.operands = [*gathers, *views, *swaps]
        anywhere = pl.BlockSpec(memory_space=pl.ANY)
        self.in_specs = [anywhere] * len(self.operands)
        rows = [view.shape[-2:] for view in views]
        self.out_specs = (
            [anywhere] * len(gathers)
            + [pl.BlockSpec(shape, lambda *at: (0, 0)) for shape in rows]
            + [anywhere] * len(swaps)
        )
        self.out_shape = (
            [jax.ShapeDtypeStruct(block_grid + shard.shape, shard.dtype) for shard in gathers]
            + [jax.ShapeDtypeStruct(shape, jnp.float32) for shape in rows]
            + [jax.ShapeDtypeStruct(values.shape, values.dtype) for values in swaps]
        )
        sizes = [where[1::2] for _, where, _ in scatter_chunks]
        self.slots = {}
        self.scratch_shapes = []
        for i, size in enumerate(sizes):
            if i < kept_slots or sizes[i - kept_slots] != size:
                self.slots[i] = len(self.scratch_shapes)
                self.scratch_shapes.append(pltpu.VMEM((4, 2, 2) + size, jnp.bfloat16))
            else:
                self.slots[i] = self.slots[i - kept_slots]
        self.kept = len(self.scratch_shapes)
        self.scratch_shapes += [pltpu.VMEM((4, 2, 2) + size, jnp.bfloat16) for size in sizes]
        extents = dict(zip("zxy", (grid_z, grid_x, grid_y)))
        for hop in range(3):
            for (_, _, order), size in zip(scatter_chunks, sizes):
                lead = [extents[order[hop]] - 1] + [extents[one] for one in "zxy" if one not in order[: hop + 1]]
                self.scratch_shapes.append(pltpu.VMEM((*lead, *size), jnp.bfloat16))
        self.scratch_shapes += [pltpu.VMEM(block_grid + shard.shape, shard.dtype) for shard in gathers]
        self.scratch_shapes += [pltpu.VMEM(values.shape, values.dtype) for values in swaps]
        for count, hops in ((len(gather_chunks), 6), (len(scatter_chunks), 6)):
            if count:
                self.scratch_shapes += [
                    pltpu.SemaphoreType.DMA((count,)),
                    pltpu.SemaphoreType.DMA((count, hops)),
                    pltpu.SemaphoreType.DMA((count, hops)),
                ]
        if swaps:
            pieces = sum(len(pieces_of(values.shape[1])) for values in swaps)
            self.scratch_shapes += [pltpu.SemaphoreType.DMA((count,)) for count in (len(swaps), pieces, pieces)]

    def steps(self, ins, outs, scratch):
        gathers, scatters, swaps = self.counts
        scratch = list(scratch)

        def take(count):
            taken = scratch[:count]
            del scratch[:count]
            return taken

        kept = take(self.kept)
        buffers = [[kept[self.slots[i]] for i in range(self.scatter_count)]]
        buffers += [take(self.scatter_count) for _ in range(4)]
        fulls, items = take(gathers), take(swaps)
        lists = []
        if gathers:
            lists.append(gather_steps(self.gather_groups, ins[:gathers], outs[:gathers], fulls, take(3)))
        if scatters:
            span = slice(gathers, gathers + scatters)
            lists.append(scatter_steps(self.scatter_groups, ins[span], outs[span], buffers, take(3)))
        if swaps:
            lists.append(swap_steps(ins[gathers + scatters :], outs[gathers + scatters :], items, take(3)))
        steps = [meet]
        for group in itertools.zip_longest(*(begin for begin, _ in lists)):
            steps.append(functools.partial(call_all, [one for one in group if one is not None]))
        steps[:2] = [functools.partial(call_all, steps[:2])]
        ends = [end[0] for _, end in lists] + [one for _, end in lists for one in end[1:]]
        steps.append(functools.partial(call_all, ends))
        return steps


def call_all(functions):
    for function in functions:
        function()


def carried(body, moves, *, grid, in_specs, out_specs, out_shape, scratch_shapes, ident, name, last=None, tail=0):
    if moves is None:
        run = pl.pallas_call(
            body,
            grid=grid,
            in_specs=in_specs,
            out_specs=out_specs,
            out_shape=out_shape,
            scratch_shapes=scratch_shapes,
            compiler_params=pltpu.CompilerParams(vmem_limit_bytes=48 * 1024 * 1024),
            name=name,
        )
        return lambda *operands: (run(*operands), ())
    counts = [len(in_specs), len(moves.in_specs), len(out_specs), len(moves.out_specs), len(scratch_shapes)]

    def kernel(*refs):
        refs = list(refs)
        parts = []
        for count in counts:
            parts.append(refs[:count])
            del refs[:count]
        ins, move_ins, outs, move_outs, scratch = parts
        steps = moves.steps(move_ins, move_outs, refs)
        size = 1
        for extent in grid:
            size *= extent
        at = pl.program_id(0)
        early = len(steps) - tail
        for i in range(size):
            group = [steps[k] for k in range(early) if k * size // early == i]
            if group:
                pl.when(at == i)(functools.partial(call_all, group))
        if body is not None:
            body(*ins, *outs, *scratch)
        late = [steps[early:]]
        if last is not None:
            late.append(last(*ins, *outs, *scratch))
        order = [one for pairs in itertools.zip_longest(*late) for one in pairs if one is not None]
        if order:
            pl.when(at == size - 1)(functools.partial(call_all, order))

    call = pl.pallas_call(
        kernel,
        grid=grid,
        in_specs=[*in_specs, *moves.in_specs],
        out_specs=[*out_specs, *moves.out_specs],
        out_shape=[*out_shape, *moves.out_shape],
        scratch_shapes=[*scratch_shapes, *moves.scratch_shapes],
        compiler_params=pltpu.CompilerParams(
            collective_id=ident, has_side_effects=True, vmem_limit_bytes=60 * 1024 * 1024
        ),
        name=name,
    )

    def run(*operands):
        results = call(*operands, *moves.operands)
        return results[: len(out_shape)], results[len(out_shape) :]

    return run


def cuts(weights, orders, most=24 * 384):
    groups = []
    for index, (rows, columns) in enumerate(weights):
        if rows % 16 == 0:
            pieces = [(row, 16, 0, columns) for row in range(0, rows, 16)]
        else:
            wide = max(most // rows // pair, 1) * pair
            pieces = [(0, rows, column, min(wide, columns - column)) for column in range(0, columns, wide)]
        for piece in pieces:
            groups.append(((index, piece, orders[len(groups) % len(orders)]),))
    return tuple(groups)


def shard_shapes(grads):
    blocks = grid_z * grid_x * grid_core * grid_y
    return [(grad.shape[0] // blocks, grad.shape[1]) for grad in grads]


def rms_backward(values, gain, grad):
    scale = lax.rsqrt(jnp.mean(values * values, axis=-1, keepdims=True) + epsilon)
    weighted = grad * gain
    inner = jnp.mean(values * weighted, axis=-1, keepdims=True)
    return scale * weighted - values * (scale * scale * scale * inner), jnp.sum(grad * values * scale, axis=0)


def fits(mesh):
    return mesh.shape["dp"] == grid_z * grid_x * grid_core and mesh.shape["seq"] == grid_y


def item_body(
    hidden,
    encoded,
    cotangent,
    w_self_qkv,
    w_self_out,
    w_cross_q,
    w_cross_kv,
    w_cross_out,
    w_ffn_in,
    w_ffn_out,
    norm_gains,
    bucket_bias_matrix,
    dec_lengths,
    ident_tags,
    ident_mask,
    bucket_ids,
):
    width = hidden.shape[2]
    heads = bucket_bias_matrix.shape[1]
    bucket_count = bucket_bias_matrix.shape[0]
    axes = ("dp", "seq")
    place = lax.axis_index("seq")
    both_ids = jnp.broadcast_to(bucket_ids.astype(jnp.bfloat16), (2,) + bucket_ids.shape)
    lanes = (jnp.arange(pair) % (pair // 2) == 0).astype(jnp.float32)
    tags = jnp.where(ident_tags[..., None] == 0, 0.0, masked_score * lanes).astype(jnp.bfloat16)
    group = (w_self_qkv, w_cross_kv, w_self_out, w_cross_q, w_cross_out)
    *weights, own_hidden, ids, tags, own_encoded = bring(
        Moves(
            group,
            cuts([weight.shape for weight in group], ["yzxc"]),
            swaps=[hidden, both_ids, tags, encoded],
        )
    )
    tag_lanes = tags.reshape(-1, pair)
    wqkv, wckv, wso, wcq, wco = (weight.reshape(width, -1) for weight in weights)
    enc_rows = own_encoded.reshape(-1, width)
    states = own_hidden.reshape(-1, width)
    ids = ids.reshape(-1, ids.shape[-1])
    length = jnp.broadcast_to(dec_lengths[:, None], (2, pair))
    marks = lax.dynamic_index_in_dim(ident_mask, place, 0, keepdims=False)
    table = jnp.concatenate(
        [
            jnp.transpose(bucket_bias_matrix),
            jnp.full((heads, pair - bucket_count), masked_score, jnp.float32),
        ],
        axis=1,
    ).reshape(heads // 2, 2, pair)
    mark_lanes = jnp.where(marks[:, None] == 1, 0.0, lanes[None, :]).astype(jnp.bfloat16)

    group = (w_ffn_in, w_ffn_out)
    kept, (slse, clse), (win, wout, own_cotangent) = attention_forward(
        length, ids, tag_lanes, mark_lanes, table, norm_gains, states, wqkv, enc_rows, wso, wcq, wckv, wco,
        Moves(group, cuts([weight.shape for weight in group], ["yzxc", "zxyc"]), swaps=[cotangent]),
    )
    win = win.reshape(width, -1)
    wout = wout.reshape(-1, width)
    grad_low = own_cotangent.reshape(-1, width)
    grad_top = grad_low.astype(jnp.float32)
    after_cross, normed_three = kept.x2, kept.n3
    pre = matmul(normed_three, win)
    act = smooth_gelu(pre).astype(jnp.bfloat16)
    block_out = (after_cross + matmul(act, wout)).astype(jnp.bfloat16)

    halves = (2, -1, width)
    grad_wout = contract_rows(act, grad_low).astype(jnp.bfloat16)
    grad_act = contract_cols(grad_low, wout)
    grad_pre = jax.vjp(smooth_gelu, pre)[1](grad_act)[0].astype(jnp.bfloat16)
    grad_win = contract_rows(normed_three, grad_pre).astype(jnp.bfloat16)
    back, gain_three = rms_backward(after_cross, norm_gains[2], contract_cols(grad_pre, win))
    grad_cross = grad_top + back
    cross_low = grad_cross.astype(jnp.bfloat16)
    grad_wco = contract_rows(kept.catt, cross_low).astype(jnp.bfloat16)
    grad_catt = contract_cols(cross_low, wco).astype(jnp.bfloat16)
    grads = [grad_wout, grad_win, grad_wco]
    outs, (sum_wout, sum_win, sum_wco, block_out) = attention_backward(
        kept.cq, kept.ckv, tag_lanes, mark_lanes, grad_catt, kept.cfull, clse,
        kept.qkv, kept.ids_t, table, kept.sfull, slse,
        norm_gains, states, kept.x1, grad_cross, kept.n1, kept.n2, kept.att, enc_rows,
        wcq, wso, wckv, wqkv,
        Moves(
            scatters=grads,
            scatter_groups=cuts(shard_shapes(grads), ["xzy", "xzy", "xzy", "yxz"]),
            swaps=[block_out.reshape(halves)],
        ),
    )
    grad_scores, grad_wqkv, grad_wckv, grad_wcq, grad_wso, grad_enc, grad_inputs, gain_rows = outs
    gains = jnp.concatenate([gain_rows[0], gain_rows[1], gain_three])
    rows = -(-gains.shape[0] // (8 * pair)) * 8
    gains = jnp.pad(gains, (0, rows * pair - gains.shape[0])).reshape(rows, pair)
    grads = [grad_wckv, grad_wcq, grad_wso, grad_wqkv]
    (small,), (sum_wckv, sum_wcq, sum_wso, sum_wqkv) = table_sums(
        gains,
        kept.ids_t,
        grad_scores,
        bucket_count,
        Moves(
            scatters=grads,
            scatter_groups=cuts(shard_shapes(grads), ["xzy", "yxz"]),
        ),
    )
    results = deliver(
        [block_out, grad_inputs, grad_enc, sum_wqkv, sum_wso, sum_wcq, sum_wckv, sum_wco, sum_win, sum_wout]
    )
    gains = small[:rows].reshape(-1)[: 3 * width].reshape(3, width)
    grad_table = small[rows:, :heads]
    return (*results, gains, grad_table)


def solution(mesh):
    placed = (
        P("dp", "seq", None),
        P("dp", "seq", None),
        P("dp", "seq", None),
        P(("dp", "seq"), None),
        P(("dp", "seq"), None),
        P(("dp", "seq"), None),
        P(("dp", "seq"), None),
        P(("dp", "seq"), None),
        P(("dp", "seq"), None),
        P(("dp", "seq"), None),
        P(),
        P(),
        P("dp"),
        P("dp", "seq"),
        P("dp", None),
        P("seq", None),
    )

    def body(*arrays):
        items = arrays[0].shape[0]
        if items == 2 and lax.axis_size("seq") == 2 and fits(mesh):
            return item_body(*arrays)
        return split_body(*arrays)

    return jax.shard_map(
        body,
        mesh=mesh,
        in_specs=placed,
        out_specs=(
            P("dp", "seq", None),
            P("dp", "seq", None),
            P("dp", "seq", None),
            P(("dp", "seq"), None),
            P(("dp", "seq"), None),
            P(("dp", "seq"), None),
            P(("dp", "seq"), None),
            P(("dp", "seq"), None),
            P(("dp", "seq"), None),
            P(("dp", "seq"), None),
            P(),
            P(),
        ),
        check_vma=False,
    )
```
